1024 devices in a mesh: gx: 128 (over y, x, core), gy: 8 (over z).
Axes of the slice: x: 8, y: 8, z: 8, core: 2. Of those that a mesh axis runs over, the one named last changes fastest.
Arguments:
- load: float32 [3, 256, 64, 128], P(None, 'gx', 'gy'), may hold values from -12 to 12
- viscous: float32 [6, 256, 64, 128], P(None, 'gx', 'gy'), may hold values from -4 to 4
- material: int32 [256, 64, 128], P('gx', 'gy'), may hold values from 0 to 15
- free_nodes: int32 [256, 64, 128], P('gx', 'gy'), may hold values 0 or 1
- moduli_table: float32 [3, 16], replicated, may hold values from 0.5 to 5
- relax_time: float32 [16], replicated, may hold values from 0.1 to 10
Outputs:
- displacement: float32 [3, 256, 64, 128], P(None, 'gx', 'gy')
- viscous_next: float32 [6, 256, 64, 128], P(None, 'gx', 'gy')
The draws below stay inside these ranges and needn't reach their ends.
All inputs are finite; a program needn't handle non-finite values. No bound on the sum of `free_nodes` on one device may be relied on, other than what follows from the above.
Results may differ from the reference program's by a relative error of at most 0.00035.
Values sent between devices are 32-bit elements; how exact they have to be, the bound alone decides.
No kernel may reach another device: no remote copies, remote signals or barrier semaphores. Data moves between devices by JAX's collectives and lax.ppermute only.
A program may use at most 64 MiB of HBM per device.

```python
import math
from functools import partial
import jax
import jax.numpy as jnp
from jax import lax

NZ = 128
CLASSES = 16
ITERS = 4
NX = 256
NY = 64


def draw_load(key, part):
    key = jax.random.fold_in(key, 11)
    along = jnp.arange(NX, dtype=jnp.float32) / max(NX - 1, 1)
    ramp = (1.0 + 2.0 * along)[None, :, None, None]
    value = ramp * jax.random.truncated_normal(key, -4.0, 4.0, (3, NX, NY, NZ), jnp.float32)
    return value.astype(jnp.float32)


def with_ends(entries, own_key, least, largest):
    extent = entries.shape
    spot = [jax.random.randint(jax.random.fold_in(own_key, axis), (), 0, extent[axis]) for axis in range(len(extent))]
    entries = entries.at[tuple(spot)].set(least)
    longest = extent.index(max(extent))
    spot[longest] = (spot[longest] + 1) % extent[longest]
    return entries.at[tuple(spot)].set(largest)


def levels(rng, extent, pieces, low, top_value):
    def one(dim, parts):
        draws = jax.random.uniform(jax.random.fold_in(jax.random.fold_in(rng, 6), dim), (parts,), jnp.float32, low / len(pieces), top_value / len(pieces))
        return jnp.repeat(jnp.exp(draws), extent[dim] // parts).reshape((-1,) + (1,) * (len(extent) - dim - 1))

    gain = one(*pieces[0])
    for cut in pieces[1:]:
        gain = gain * one(*cut)
    return gain


def noise(own_key, extent, width, most, split=(), kind=jnp.bfloat16):
    loudness = levels(own_key, extent, split, -0.22, 0.18) if split else 1.0
    result = jax.random.normal(own_key, extent, jnp.float32) * width * loudness
    return jnp.minimum(jnp.maximum(result, -most), most).astype(kind)


def setup_inputs(seed: int = 0) -> dict:
    keys = jax.random.split(jax.random.key(seed), 7)
    return {
        "load": draw_load(jax.random.fold_in(keys[6], 71), 0),
        "viscous": noise(keys[1], (6, NX, NY, NZ), 0.5, 4.0, ((1, 128), (2, 8)), jnp.float32),
        "material": with_ends(jax.random.randint(keys[2], (NX, NY, NZ), 0, CLASSES), jax.random.fold_in(keys[2], 1), 0, CLASSES - 1).astype(jnp.int32),
        "free_nodes": with_ends((jax.random.randint(keys[3], (NX, NY, NZ), 0, 8) < 7).astype(jnp.int32), jax.random.fold_in(keys[3], 1), 0, 1),
        "moduli_table": jnp.clip(jnp.exp(jax.random.uniform(keys[4], (3, CLASSES), jnp.float32, math.log(0.5), math.log(5.0))), 0.5, 5.0),
        "relax_time": jnp.clip(jnp.exp(jax.random.uniform(keys[5], (CLASSES,), jnp.float32, math.log(0.1), math.log(10.0))), 0.1, 10.0),
    }


GAUSS_LOW = 0.5 - 0.5 / math.sqrt(3.0)
GAUSS_POINTS = (GAUSS_LOW, 1.0 - GAUSS_LOW)
CENTROID = (0.5, 0.5, 0.5)

def blend(field, axis, weight):
    length = field.shape[axis]
    lower = lax.slice_in_dim(field, 0, length - 1, axis=axis)
    upper = lax.slice_in_dim(field, 1, length, axis=axis)
    if weight is None:
        return upper - lower
    return (1.0 - weight) * lower + weight * upper

def point_strain(nodes, point):
    first, second, third = point
    along_x = blend(blend(blend(nodes, 1, None), 2, second), 3, third)
    along_y = blend(blend(blend(nodes, 1, first), 2, None), 3, third)
    along_z = blend(blend(blend(nodes, 1, first), 2, second), 3, None)
    return jnp.stack([along_x[0], along_y[1], along_z[2], 0.5 * (along_y[2] + along_z[1]), 0.5 * (along_x[2] + along_z[0]), 0.5 * (along_x[1] + along_y[0])])

def elastic_load(strain, lame_first, shear, weight):
    trace = strain[0] + strain[1] + strain[2]
    normal_part = weight * (lame_first * trace + 2.0 * shear * strain[:3])
    shear_part = weight * 4.0 * shear * strain[3:]
    return jnp.concatenate([normal_part, shear_part], axis=0)

def arm_load(strain, shear_arm):
    return jnp.concatenate([2.0 * shear_arm * strain[:3], 4.0 * shear_arm * strain[3:]], axis=0)

def element_forces(nodes, lame_first, shear_inf, shear_arm):
    total = jnp.zeros_like(nodes)
    for first in GAUSS_POINTS:
        for second in GAUSS_POINTS:
            for third in GAUSS_POINTS:
                strain, pullback = jax.vjp(partial(point_strain, point=(first, second, third)), nodes)
                total = total + pullback(elastic_load(strain, lame_first, shear_inf, 0.125))[0]
    strain, pullback = jax.vjp(partial(point_strain, point=CENTROID), nodes)
    return total + pullback(arm_load(strain, shear_arm))[0]

def history_forces(viscous, shear_arm, nodes_shape):
    blank = jnp.zeros(nodes_shape, viscous.dtype)
    strain, pullback = jax.vjp(partial(point_strain, point=CENTROID), blank)
    return pullback(arm_load(viscous, shear_arm))[0]

def reference(load, viscous, material, free_nodes, moduli_table, relax_time):
    retain_class = relax_time / (relax_time + 1.0)
    lame_first = moduli_table[0][material]
    shear_inf = moduli_table[1][material]
    retain = retain_class[material]
    shear_arm = moduli_table[2][material] * retain
    mask = free_nodes.astype(load.dtype)

    def widen(field):
        return jnp.pad(field, ((0, 0), (1, 0), (1, 0), (0, 1)))

    def narrow(forces):
        return forces[:, 1:, 1:, :-1]

    def operator(field):
        masked = mask * field
        forces = narrow(element_forces(widen(masked), lame_first, shear_inf, shear_arm))
        return mask * forces + (1.0 - mask) * field
    history = narrow(history_forces(viscous, shear_arm, widen(load).shape))
    right = mask * (load + history)
    displacement = jnp.zeros_like(load)
    residual = right
    image = operator(residual)
    norm_now = jnp.sum(residual * residual)
    curvature = jnp.sum(residual * image)
    alpha = norm_now / curvature
    direction, along = (residual, image)
    for step in range(ITERS):
        displacement = displacement + alpha * direction
        residual = residual - alpha * along
        if step + 1 < ITERS:
            image = operator(residual)
            norm_next = jnp.sum(residual * residual)
            curvature = jnp.sum(residual * image)
            ratio = norm_next / norm_now
            alpha = norm_next / (curvature - ratio * norm_next / alpha)
            direction = residual + ratio * direction
            along = image + ratio * along
            norm_now = norm_next
    centre = point_strain(widen(displacement), CENTROID)
    viscous_next = retain * viscous + (1.0 - retain) * centre
    return (displacement, viscous_next)
```

```python
import math

import jax
import jax.numpy as jnp
from jax import lax
from jax.experimental import pallas as pl
from jax.experimental.pallas import tpu as pltpu
from jax.sharding import Mesh, PartitionSpec as P

ITERS = 4
ROWS = 16
LAYERS = 10
FIELDS = 11
CLASSES = 16
TINY_PIVOT = 1e-6

F32 = jnp.float32
SDS = jax.ShapeDtypeStruct
VMEM = pl.BlockSpec(memory_space=pltpu.VMEM)
SMEM = pl.BlockSpec(memory_space=pltpu.SMEM)
PAIRS = ("ss", "sd", "ds", "dd")


def call(body, out_shape, n_in, scratch=(), first_scalar=False, flops=100000):
    specs = [VMEM] * n_in
    if first_scalar:
        specs[0] = SMEM
    many = isinstance(out_shape, (list, tuple))
    return pl.pallas_call(
        body,
        out_shape=out_shape,
        in_specs=specs,
        out_specs=[VMEM] * len(out_shape) if many else VMEM,
        scratch_shapes=list(scratch),
        compiler_params=pltpu.CompilerParams(vmem_limit_bytes=24 * 1024 * 1024),
        cost_estimate=pl.CostEstimate(flops=flops, bytes_accessed=100000, transcendentals=0),
    )


def pack_body(load, viscous, material, free, moduli, relax, own, low, high, table):
    for field in range(FIELDS):
        layers = []
        for layer in range(2):
            if field < 3:
                tile = load[field, layer]
            elif field < 9:
                tile = viscous[field - 3, layer]
            elif field == 9:
                tile = material[layer].astype(F32) - float(CLASSES)
            else:
                tile = free[layer].astype(F32)
            own[2 * field + layer] = tile
            layers.append(tile)
        row = lax.broadcasted_iota(jnp.int32, (8, 128), 0)
        low[field] = jnp.where(row < 4, layers[0], pltpu.roll(layers[1], 4, 0))
        high[field] = jnp.where(row < 4, pltpu.roll(layers[0], 4, 0), layers[1])
    time = relax[...]
    retain = time / (time + 1.0)
    arm = moduli[2:3] * retain
    bound = jnp.max(moduli[0:1] + 2.0 * (moduli[1:2] + arm), axis=1, keepdims=True)
    table[...] = jnp.zeros((8, 128), F32)
    table[0:1, 0:CLASSES] = moduli[0:1] * (1.0 / 16.0)
    table[1:2, 0:CLASSES] = moduli[1:2] * (1.0 / 16.0)
    table[2:3, 0:CLASSES] = arm * (1.0 / 16.0)
    table[3:4, 0:CLASSES] = retain
    table[4:5] = jnp.broadcast_to(1.0 / bound, (1, 128))


def widen_body(own, above, below, wide):
    row = lax.broadcasted_iota(jnp.int32, (8, 128), 0)
    for field in range(FIELDS):
        upper, lower = above[field], below[field]
        uppers = (upper, pltpu.roll(upper, 4, 0))
        lowers = (pltpu.roll(lower, 4, 0), lower)
        for layer in range(2):
            k = 2 * field + layer
            wide[k, 0:8] = own[k]
            wide[k, 8:16] = jnp.where(row < 4, uppers[layer], lowers[layer])


def choose_body(core, wide, left, right, out):
    @pl.when(core[0] == 0)
    def _():
        out[0] = wide[...]
        out[1] = right[...]

    @pl.when(core[0] != 0)
    def _():
        out[0] = left[...]
        out[1] = wide[...]


def iota(axis, shape=(ROWS, 128)):
    return lax.broadcasted_iota(jnp.int32, shape, axis)


def next_lane(tile):
    return jnp.where(iota(1) < 127, pltpu.roll(tile, 127, 1), 0.0)


def previous_lane(tile):
    return jnp.where(iota(1) > 0, pltpu.roll(tile, 1, 1), 0.0)


def node_pairs(tile, last=True):
    lower = pltpu.roll(tile, 1, 0)
    parts = {}
    for name, part in (("s", tile + lower), ("d", tile - lower)):
        upper = next_lane(part)
        parts[name + "s"] = part + upper
        if last or name == "s":
            parts[name + "d"] = upper - part
    return parts


def element_modes(lower, upper):
    modes = []
    for below, above in zip(lower, upper):
        mode = {"d" + pair: above[pair] - below[pair] for pair in above}
        mode.update({"s" + pair: above[pair] + below[pair] for pair in above if pair != "ss"})
        modes.append(mode)
    return modes


def element_loads(modes, moduli):
    lame, both, lame_third, shear_third, cubic = moduli
    u, v, w = modes
    fu, fv, fw = {}, {}, {}
    trace = lame * (u["dss"] + v["sds"] + w["ssd"])
    twice = both + both
    fu["dss"] = trace + twice * u["dss"]
    fv["sds"] = trace + twice * v["sds"]
    fw["ssd"] = trace + twice * w["ssd"]
    fw["sds"] = fv["ssd"] = both * (w["sds"] + v["ssd"])
    fw["dss"] = fu["ssd"] = both * (w["dss"] + u["ssd"])
    fv["dss"] = fu["sds"] = both * (v["dss"] + u["sds"])
    triple = 3.0 * shear_third
    part = lame_third * (u["dds"] + w["sdd"])
    fu["dds"] = part + triple * u["dds"]
    fw["sdd"] = part + triple * w["sdd"]
    part = lame_third * (v["dds"] + w["dsd"])
    fv["dds"] = part + triple * v["dds"]
    fw["dsd"] = part + triple * w["dsd"]
    part = lame_third * (u["dsd"] + v["sdd"])
    fu["dsd"] = part + triple * u["dsd"]
    fv["sdd"] = part + triple * v["sdd"]
    part = w["dds"] + v["dsd"] + u["sdd"]
    fw["dds"] = shear_third * (part + w["dds"])
    fv["dsd"] = shear_third * (part + v["dsd"])
    fu["sdd"] = shear_third * (part + u["sdd"])
    for mode, force in zip(modes, (fu, fv, fw)):
        force["ddd"] = cubic * mode["ddd"]
    return fu, fv, fw


def plus(a, b):
    return b if a is None else a if b is None else a + b


def to_nodes(forces):
    uppers, lowers = [], []
    for force in forces:
        upper, lower = {}, {}
        for pair in PAIRS:
            s, d = force.get("s" + pair), force.get("d" + pair)
            upper[pair] = plus(s, d)
            lower[pair] = None if s is None and d is None else (-d if s is None else s if d is None else s - d)
        uppers.append(upper)
        lowers.append(lower)
    return uppers, lowers


def node_force(pairs):
    along = {}
    for name in "sd":
        s, d = pairs[name + "s"], pairs[name + "d"]
        if d is None:
            along[name] = s + previous_lane(s)
        else:
            along[name] = (s - d) + previous_lane(s + d)
    return (along["s"] + along["d"]) + pltpu.roll(along["s"] - along["d"], ROWS - 1, 0)


def merged(first, second):
    return [{pair: plus(a[pair], b[pair]) for pair in PAIRS} for a, b in zip(first, second)]


def pick(table, row, index):
    entries = jnp.broadcast_to(table[row : row + 1], (ROWS, 128))
    return jnp.take_along_axis(entries, index, axis=1, mode="promise_in_bounds")


def krylov_body(left, rec, wide, right, table, basis, sums, vec, mask, moduli, images):
    blocks = (left, rec.at[0], wide, rec.at[1], right)

    def field(number, layer):
        return blocks[layer // 2][2 * number + layer % 2]

    pending = None
    for layer in range(LAYERS):
        index = field(9, layer).astype(jnp.int32) + CLASSES
        lame, shear, arm = (pick(table, row, index) for row in range(3))
        moduli[0, layer] = lame
        moduli[1, layer] = shear + arm
        moduli[2, layer] = lame * (1.0 / 3.0)
        moduli[3, layer] = shear * (1.0 / 3.0)
        moduli[4, layer] = (lame + 4.0 * shear) * (1.0 / 9.0)
        mask[layer] = field(10, layer)
        factor = 8.0 * arm
        xx, yy, zz, yz, xz, xy = (factor * field(3 + part, layer) for part in range(6))
        forces = (
            {"dss": xx, "ssd": xz, "sds": xy},
            {"sds": yy, "ssd": yz, "dss": xy},
            {"ssd": zz, "sds": yz, "dss": xz},
        )
        upper, lower = to_nodes(forces)
        if pending is not None:
            node = layer - 1
            for comp, pairs in enumerate(merged(pending, lower)):
                vec[0, comp, node] = mask[node] * (field(comp, node) + node_force(pairs))
        pending = upper

    scale = jnp.broadcast_to(table[4:5], (ROWS, 128))

    def masked_pairs(step, layer):
        return [node_pairs(mask[layer] * vec[step, comp, layer]) for comp in range(3)]

    for step in range(ITERS - 1):
        below = masked_pairs(step, step)
        pending = None
        for layer in range(step + 1, LAYERS - 1 - step):
            above = masked_pairs(step, layer)
            loads = element_loads(element_modes(below, above), [moduli[k, layer] for k in range(5)])
            upper, lower = to_nodes(loads)
            if pending is not None:
                node = layer - 1
                free = mask[node]
                for comp, pairs in enumerate(merged(pending, lower)):
                    value = vec[step, comp, node]
                    image = free * node_force(pairs) + (1.0 - free) * value
                    if node in (4, 5):
                        images[step, comp, node - 4] = image[0:8]
                    if step == 0:
                        fresh = scale * image - value
                    else:
                        fresh = 2.0 * (scale * image - value) - vec[step - 1, comp, node]
                    vec[step + 1, comp, node] = fresh
            pending = upper
            below = above

    last = ITERS - 1
    energy = jnp.zeros((8, 128), F32)
    below = masked_pairs(last, 3)
    for layer in (4, 5):
        above = masked_pairs(last, layer)
        modes = element_modes(below, above)
        loads = element_loads(modes, [moduli[k, layer] for k in range(5)])
        total = None
        for mode, force in zip(modes, loads):
            for name in force:
                total = plus(total, (mode[name] * force[name])[0:8])
        energy = energy + total
        for comp in range(3):
            value = vec[last, comp, layer, 0:8]
            energy = energy + (1.0 - mask[layer, 0:8]) * value * value
        below = above

    def product(first, second):
        total = None
        for comp in range(3):
            for layer in range(2):
                total = plus(total, first(comp, layer) * second(comp, layer))
        return total

    def vector(step):
        return lambda comp, layer: vec[step, comp, 4 + layer, 0:8]

    def image(step):
        return lambda comp, layer: images[step, comp, layer]

    products = []
    for i in range(ITERS):
        for j in range(i + 1):
            if i == last and j == last:
                products.append(energy)
            elif i == last:
                products.append(product(vector(i), image(j)))
            else:
                products.append(product(vector(j), image(i)))
    for i in range(ITERS):
        products.append(product(vector(0), vector(i)))
    rows = jnp.zeros((ROWS, 128), F32)
    for number, value in enumerate(products):
        rows = jnp.where(iota(0) == number, jnp.sum(value, axis=0, keepdims=True), rows)
    column = jnp.sum(rows, axis=1, keepdims=True)
    line = jnp.sum(jnp.where(iota(0) == iota(1), column, 0.0), axis=0, keepdims=True)
    sums[...] = jnp.broadcast_to(line, sums.shape)
    for step in range(ITERS):
        for comp in range(3):
            for layer in range(3):
                basis[step, comp, layer] = vec[step, comp, 3 + layer]


def final_body(sums, basis, own, table, displacement, viscous_next):
    line = jnp.sum(sums[...], axis=0, keepdims=True)
    lane = iota(1, (1, 128))

    def entry(number):
        return jnp.sum(jnp.where(lane == number, line, 0.0), axis=1, keepdims=True)

    matrix = [[entry(i * (i + 1) // 2 + j) for j in range(i + 1)] for i in range(ITERS)]
    value = [entry(10 + i) for i in range(ITERS)]
    first = [matrix[i][i] for i in range(ITERS)]
    ratio = {}
    inverse = []
    for k in range(ITERS):
        pivot = matrix[k][k]
        inverse.append(jnp.where(pivot > TINY_PIVOT * first[k], 1.0 / pivot, 0.0))
        for i in range(k + 1, ITERS):
            ratio[i, k] = matrix[i][k] * inverse[k]
            for j in range(k + 1, i + 1):
                matrix[i][j] = matrix[i][j] - ratio[i, k] * matrix[j][k]
            value[i] = value[i] - ratio[i, k] * value[k]
    value = [value[k] * inverse[k] for k in range(ITERS)]
    for k in reversed(range(ITERS)):
        for i in range(k):
            value[i] = value[i] - ratio[k, i] * value[k]
    weights = [jnp.broadcast_to(v, (ROWS, 128)) for v in value]

    pairs = []
    for layer in range(3):
        fields = []
        for comp in range(3):
            total = weights[0] * basis[0, comp, layer]
            for step in range(1, ITERS):
                total = total + weights[step] * basis[step, comp, layer]
            if layer > 0:
                displacement[comp, layer - 1] = total[0:8]
            fields.append(node_pairs(total, last=False))
        pairs.append(fields)
    for layer in range(2):
        u, v, w = element_modes(pairs[layer], pairs[layer + 1])
        strain = (
            0.25 * u["dss"],
            0.25 * v["sds"],
            0.25 * w["ssd"],
            0.125 * (w["sds"] + v["ssd"]),
            0.125 * (w["dss"] + u["ssd"]),
            0.125 * (v["dss"] + u["sds"]),
        )
        index = own[18 + layer].astype(jnp.int32) + CLASSES
        entries = jnp.broadcast_to(table[3:4], (8, 128))
        retain = jnp.take_along_axis(entries, index, axis=1, mode="promise_in_bounds")
        for part in range(6):
            old = own[6 + 2 * part + layer]
            viscous_next[part, layer] = retain * old + (1.0 - retain) * strain[part][0:8]


def shifted(value, axes, count, steps):
    pairs = [(i, i + steps) for i in range(count) if 0 <= i + steps < count]
    return lax.ppermute(value, axes, pairs)


def summed(value, axes):
    return jnp.sum(lax.all_to_all(value, axes, 0, 0), axis=0)


def solution(mesh):
    count_x, count_z = mesh.shape["gx"], mesh.shape["gy"]
    along = min(8, count_x // 2)
    across = count_x // (2 * along)
    grid = Mesh(mesh.devices.reshape(across, along, 2, count_z), ("y", "x", "core", "z"))
    chips = along * across

    def shards(load, viscous, material, free_nodes, moduli_table, relax_time):
        own, low, high, table = call(
            pack_body,
            (SDS((22, 8, 128), F32), SDS((11, 8, 128), F32), SDS((11, 8, 128), F32), SDS((8, 128), F32)),
            6,
        )(load, viscous, material, free_nodes, moduli_table, relax_time.reshape(1, -1))
        below = shifted(high, ("z",), count_z, 1)
        above = shifted(low, ("z",), count_z, -1)
        wide = call(widen_body, SDS((22, ROWS, 128), F32), 3)(own, above, below)
        left = shifted(wide, ("y", "x"), chips, 1)
        right = shifted(wide, ("y", "x"), chips, -1)
        core = lax.axis_index("core").astype(jnp.int32).reshape(1)
        given = call(choose_body, SDS((2, 22, ROWS, 128), F32), 4, first_scalar=True)(core, wide, left, right)
        taken = lax.ppermute(given, ("core",), [(0, 1), (1, 0)])
        near, far = 2 * along, across * count_z
        basis, sums = call(
            krylov_body,
            (SDS((ITERS, 3, 3, ROWS, 128), F32), SDS((near, 128), F32)),
            5,
            scratch=(
                pltpu.VMEM((ITERS, 3, LAYERS, ROWS, 128), F32),
                pltpu.VMEM((LAYERS, ROWS, 128), F32),
                pltpu.VMEM((5, LAYERS, ROWS, 128), F32),
                pltpu.VMEM((ITERS - 1, 3, 2, 8, 128), F32),
            ),
            flops=20000000,
        )(left, taken, wide, right, table)
        partial = summed(sums.reshape(near, 1, 128), ("x", "core"))
        everything = lax.all_to_all(jnp.broadcast_to(partial[None], (far, 1, 128)), ("y", "z"), 0, 0)
        return tuple(
            call(final_body, (SDS((3, 2, 8, 128), F32), SDS((6, 2, 8, 128), F32)), 4)(
                everything.reshape(far, 128), basis, own, table
            )
        )

    return jax.shard_map(
        shards,
        mesh=grid,
        in_specs=(
            P(None, ("y", "x", "core"), "z", None),
            P(None, ("y", "x", "core"), "z", None),
            P(("y", "x", "core"), "z", None),
            P(("y", "x", "core"), "z", None),
            P(),
            P(),
        ),
        out_specs=(P(None, ("y", "x", "core"), "z", None), P(None, ("y", "x", "core"), "z", None)),
        check_vma=False,
    )
```

```python
import math

import jax
import jax.numpy as jnp
from jax import lax
from jax.experimental import pallas as pl
from jax.experimental.pallas import tpu as pltpu
from jax.sharding import Mesh, PartitionSpec as P

ITERS = 4
ROWS = 16
LAYERS = 10
FIELDS = 11
BLOCK = 13
CLASSES = 16
MOMENTS = 2 * ITERS
SCALE = 1.0 / 32.0
TINY_PIVOT = 1e-9

F32 = jnp.float32
SDS = jax.ShapeDtypeStruct
VMEM = pl.BlockSpec(memory_space=pltpu.VMEM)
SMEM = pl.BlockSpec(memory_space=pltpu.SMEM)
HBM = pl.BlockSpec(memory_space=pltpu.HBM)
PAIRS = ("ss", "sd", "ds", "dd")


def call(body, out_shape, n_in, scratch=(), first=None, flops=100000):
    specs = [VMEM] * n_in if first is not HBM else [HBM] * n_in
    if first is SMEM:
        specs[0] = SMEM
    many = isinstance(out_shape, (list, tuple))
    return pl.pallas_call(
        body,
        out_shape=out_shape,
        in_specs=specs,
        out_specs=[VMEM] * len(out_shape) if many else VMEM,
        scratch_shapes=list(scratch),
        compiler_params=pltpu.CompilerParams(vmem_limit_bytes=24 * 1024 * 1024),
        cost_estimate=pl.CostEstimate(flops=flops, bytes_accessed=100000, transcendentals=0),
    )


def pack_body(load, viscous, material, free, moduli, relax, own, low, high, table, kinds, frees, entries, times, done):
    pairs = (
        (load, own.at[0:6]),
        (viscous, own.at[6:18]),
        (material, kinds),
        (free, frees),
        (moduli, entries),
        (relax, times),
    )
    copies = [pltpu.make_async_copy(source, target, done.at[k]) for k, (source, target) in enumerate(pairs)]
    for copy in copies:
        copy.start()
    for copy in copies:
        copy.wait()
    row = lax.broadcasted_iota(jnp.int32, (8, 128), 0)
    for field in range(FIELDS):
        if field == 9:
            layers = [kinds[layer].astype(F32) - float(CLASSES) for layer in range(2)]
        elif field == 10:
            layers = [frees[layer].astype(F32) for layer in range(2)]
        else:
            layers = [own[2 * field + layer] for layer in range(2)]
        if field >= 9:
            for layer in range(2):
                own[2 * field + layer] = layers[layer]
        low[field] = jnp.where(row < 4, layers[0], pltpu.roll(layers[1], 4, 0))
        high[field] = jnp.where(row < 4, pltpu.roll(layers[0], 4, 0), layers[1])
    time = times[...]
    retain = time / (time + 1.0)
    table[...] = jnp.zeros((8, 128), F32)
    table[0:1, 0:CLASSES] = entries[0:1] * (1.0 / 16.0)
    table[1:2, 0:CLASSES] = entries[1:2] * (1.0 / 16.0)
    table[2:3, 0:CLASSES] = (entries[2:3] * retain) * (1.0 / 16.0)
    table[3:4, 0:CLASSES] = retain


def pick(table, row, index):
    entries = jnp.broadcast_to(table[row : row + 1], index.shape)
    return jnp.take_along_axis(entries, index, axis=1, mode="promise_in_bounds")


def widen_body(own, above, below, table, wide):
    row = lax.broadcasted_iota(jnp.int32, (8, 128), 0)

    def rows(field):
        upper, lower = above[field], below[field]
        halos = (
            jnp.where(row < 4, upper, pltpu.roll(lower, 4, 0)),
            jnp.where(row < 4, pltpu.roll(upper, 4, 0), lower),
        )
        return [jnp.concatenate([own[2 * field + layer], halos[layer]], axis=0) for layer in range(2)]

    fields = [rows(field) for field in range(FIELDS)]
    for layer in range(2):
        wide[9 + layer] = fields[9][layer]
        wide[11 + layer] = fields[10][layer]
    pending = None
    for layer in range(2):
        index = fields[9][layer].astype(jnp.int32) + CLASSES
        factor = 8.0 * pick(table, 2, index)
        xx, yy, zz, yz, xz, xy = (factor * fields[3 + part][layer] for part in range(6))
        forces = (
            {"dss": xx, "ssd": xz, "sds": xy},
            {"sds": yy, "ssd": yz, "dss": xy},
            {"ssd": zz, "sds": yz, "dss": xz},
        )
        upper, lower = to_nodes(forces)
        pairs = lower if pending is None else merged(pending, lower)
        for comp in range(3):
            force = node_force(pairs[comp])
            wide[3 * comp + layer] = force if layer == 0 else fields[comp][0] + force
        pending = upper
    for comp in range(3):
        wide[3 * comp + 2] = fields[comp][1] + node_force(pending[comp])


def choose_body(core, wide, left, right, out):
    @pl.when(core[0] == 0)
    def _():
        out[0] = wide[...]
        out[1] = right[...]

    @pl.when(core[0] != 0)
    def _():
        out[0] = left[...]
        out[1] = wide[...]


def iota(axis, shape=(ROWS, 128)):
    return lax.broadcasted_iota(jnp.int32, shape, axis)


def next_lane(tile):
    return jnp.where(iota(1) < 127, pltpu.roll(tile, 127, 1), 0.0)


def previous_lane(tile):
    return jnp.where(iota(1) > 0, pltpu.roll(tile, 1, 1), 0.0)


def node_pairs(tile, last=True):
    lower = pltpu.roll(tile, 1, 0)
    parts = {}
    for name, part in (("s", tile + lower), ("d", tile - lower)):
        upper = next_lane(part)
        parts[name + "s"] = part + upper
        if last or name == "s":
            parts[name + "d"] = upper - part
    return parts


def element_modes(lower, upper):
    modes = []
    for below, above in zip(lower, upper):
        mode = {"d" + pair: above[pair] - below[pair] for pair in above}
        mode.update({"s" + pair: above[pair] + below[pair] for pair in above if pair != "ss"})
        modes.append(mode)
    return modes


def element_loads(modes, moduli):
    lame, both, lame_third, shear_third, cubic = moduli
    u, v, w = modes
    fu, fv, fw = {}, {}, {}
    trace = lame * (u["dss"] + v["sds"] + w["ssd"])
    twice = both + both
    fu["dss"] = trace + twice * u["dss"]
    fv["sds"] = trace + twice * v["sds"]
    fw["ssd"] = trace + twice * w["ssd"]
    fw["sds"] = fv["ssd"] = both * (w["sds"] + v["ssd"])
    fw["dss"] = fu["ssd"] = both * (w["dss"] + u["ssd"])
    fv["dss"] = fu["sds"] = both * (v["dss"] + u["sds"])
    triple = 3.0 * shear_third
    part = lame_third * (u["dds"] + w["sdd"])
    fu["dds"] = part + triple * u["dds"]
    fw["sdd"] = part + triple * w["sdd"]
    part = lame_third * (v["dds"] + w["dsd"])
    fv["dds"] = part + triple * v["dds"]
    fw["dsd"] = part + triple * w["dsd"]
    part = lame_third * (u["dsd"] + v["sdd"])
    fu["dsd"] = part + triple * u["dsd"]
    fv["sdd"] = part + triple * v["sdd"]
    part = w["dds"] + v["dsd"] + u["sdd"]
    fw["dds"] = shear_third * (part + w["dds"])
    fv["dsd"] = shear_third * (part + v["dsd"])
    fu["sdd"] = shear_third * (part + u["sdd"])
    for mode, force in zip(modes, (fu, fv, fw)):
        force["ddd"] = cubic * mode["ddd"]
    return fu, fv, fw


def plus(a, b):
    return b if a is None else a if b is None else a + b


def to_nodes(forces):
    uppers, lowers = [], []
    for force in forces:
        upper, lower = {}, {}
        for pair in PAIRS:
            s, d = force.get("s" + pair), force.get("d" + pair)
            upper[pair] = plus(s, d)
            lower[pair] = None if s is None and d is None else (-d if s is None else s if d is None else s - d)
        uppers.append(upper)
        lowers.append(lower)
    return uppers, lowers


def node_force(pairs):
    along = {}
    for name in "sd":
        s, d = pairs[name + "s"], pairs[name + "d"]
        if d is None:
            along[name] = s + previous_lane(s)
        else:
            along[name] = (s - d) + previous_lane(s + d)
    return (along["s"] + along["d"]) + pltpu.roll(along["s"] - along["d"], ROWS - 1, 0)


def merged(first, second):
    return [{pair: plus(a[pair], b[pair]) for pair in PAIRS} for a, b in zip(first, second)]


def krylov_body(left, rec, wide, right, table, basis, sums, vec, mask, moduli):
    blocks = (left, rec.at[0], wide, rec.at[1], right)
    for layer in range(LAYERS):
        block, place = blocks[layer // 2], layer % 2
        index = block[9 + place].astype(jnp.int32) + CLASSES
        lame, shear, arm = (pick(table, row, index) for row in range(3))
        moduli[0, layer] = lame
        moduli[1, layer] = shear + arm
        moduli[2, layer] = lame * (1.0 / 3.0)
        moduli[3, layer] = shear * (1.0 / 3.0)
        moduli[4, layer] = (lame + 4.0 * shear) * (1.0 / 9.0)
        mask[layer] = block[11 + place]
        if layer < LAYERS - 1:
            for comp in range(3):
                force = block[3 * comp + 1 + place]
                if place == 1:
                    force = force + blocks[layer // 2 + 1][3 * comp]
                vec[0, comp, layer] = mask[layer] * force

    def masked_pairs(step, layer):
        return [node_pairs(mask[layer] * vec[step, comp, layer]) for comp in range(3)]

    for step in range(ITERS - 1):
        below = masked_pairs(step, step)
        pending = None
        for layer in range(step + 1, LAYERS - 1 - step):
            above = masked_pairs(step, layer)
            loads = element_loads(element_modes(below, above), [moduli[k, layer] for k in range(5)])
            upper, lower = to_nodes(loads)
            if pending is not None:
                node = layer - 1
                free = mask[node]
                for comp, pairs in enumerate(merged(pending, lower)):
                    value = vec[step, comp, node]
                    image = free * node_force(pairs) + (1.0 - free) * value
                    vec[step + 1, comp, node] = SCALE * image
            pending = upper
            below = above

    last = ITERS - 1
    energy = jnp.zeros((8, 128), F32)
    below = masked_pairs(last, 3)
    for layer in (4, 5):
        above = masked_pairs(last, layer)
        modes = element_modes(below, above)
        loads = element_loads(modes, [moduli[k, layer] for k in range(5)])
        total = None
        for mode, force in zip(modes, loads):
            for name in force:
                total = plus(total, (mode[name] * force[name])[0:8])
        energy = energy + total
        for comp in range(3):
            value = vec[last, comp, layer, 0:8]
            energy = energy + (1.0 - mask[layer, 0:8]) * value * value
        below = above

    moments = []
    for k in range(MOMENTS - 1):
        total = None
        for comp in range(3):
            for layer in (4, 5):
                total = plus(total, vec[k // 2, comp, layer, 0:8] * vec[(k + 1) // 2, comp, layer, 0:8])
        moments.append(total)
    moments.append(SCALE * energy)
    row, lane = iota(0, (8, 128)), iota(1, (8, 128))
    rows = jnp.zeros((8, 128), F32)
    for k, total in enumerate(moments):
        rows = jnp.where(row == k, jnp.sum(total, axis=0, keepdims=True), rows)
    for step in (64, 32, 16):
        rows = rows + pltpu.roll(rows, step, 1)
    line = jnp.sum(jnp.where(lane // 16 == row, rows, 0.0), axis=0, keepdims=True)
    sums[...] = jnp.broadcast_to(line, sums.shape)
    for step in range(ITERS):
        for comp in range(3):
            for layer in range(3):
                basis[step, comp, layer] = vec[step, comp, 3 + layer]


def two_sum(a, b):
    total = a + b
    part = total - a
    return total, (a - (total - part)) + (b - part)


def settle(high, low):
    total = high + low
    return total, low - (total - high)


def add(a, b):
    total, rest = two_sum(a[0], b[0])
    return settle(total, rest + (a[1] + b[1]))


def halves(a):
    wide = 4097.0 * a
    high = wide - (wide - a)
    return high, a - high


def two_product(a, b):
    total = a * b
    (ah, al), (bh, bl) = halves(a), halves(b)
    return total, ((ah * bh - total) + ah * bl + al * bh) + al * bl


def multiply(a, b):
    total, rest = two_product(a[0], b[0])
    return settle(total, rest + (a[0] * b[1] + a[1] * b[0]))


def subtract(a, b):
    return add(a, (-b[0], -b[1]))


def invert(a):
    first = 1.0 / a[0]
    total, rest = two_product(a[0], first)
    return settle(first, first * (((1.0 - total) - rest) - a[1] * first))


def rolled(a, steps, axis):
    return tuple(pltpu.roll(part, steps, axis) for part in a)


def over_rows(pair):
    for step in (4, 2, 1):
        pair = add(pair, rolled(pair, step, 0))
    return pair


def total_of(pairs):
    while len(pairs) > 1:
        pairs = [add(*pairs[k : k + 2]) if k + 1 < len(pairs) else pairs[k] for k in range(0, len(pairs), 2)]
    return pairs[0]


def middle_body(sums, out):
    pair = over_rows(total_of([(sums[k : k + 8], jnp.zeros((8, 128), F32)) for k in range(0, sums.shape[0], 8)]))
    high, low = add(pair, rolled(pair, 120, 1))
    line = jnp.where(iota(1, (8, 128)) % 16 < 8, high, pltpu.roll(low, 8, 1))
    for k in range(0, out.shape[0], 8):
        count = min(8, out.shape[0] - k)
        out[k : k + count] = line[0:count]


def final_body(sums, basis, own, table, displacement, viscous_next):
    pairs = []
    for k in range(sums.shape[0] // 8):
        tile = sums[8 * k : 8 * k + 8]
        pairs.append((tile, pltpu.roll(tile, 120, 1)))
    pair = over_rows(total_of(pairs))
    for step in (4, 2, 1):
        pair = add(pair, rolled(pair, 128 - step, 1))

    def moment(k):
        index = jnp.full((8, 128), 16 * k, jnp.int32)
        return tuple(jnp.take_along_axis(part, index, axis=1, mode="promise_in_bounds") for part in pair)

    moments = [moment(k) for k in range(MOMENTS)]
    matrix = [[moments[i + j + 1] for j in range(i + 1)] for i in range(ITERS)]
    value = moments[:ITERS]
    ratio = {}
    inverse = []
    for k in range(ITERS):
        pivot = matrix[k][k]
        kept = pivot[0] > TINY_PIVOT * moments[2 * k + 1][0]
        inverse.append(tuple(jnp.where(kept, part, 0.0) for part in invert(pivot)))
        for i in range(k + 1, ITERS):
            ratio[i, k] = multiply(matrix[i][k], inverse[k])
            for j in range(k + 1, i + 1):
                matrix[i][j] = subtract(matrix[i][j], multiply(ratio[i, k], matrix[j][k]))
            value[i] = subtract(value[i], multiply(ratio[i, k], value[k]))
    value = [multiply(value[k], inverse[k]) for k in range(ITERS)]
    for k in reversed(range(ITERS)):
        for i in range(k):
            value[i] = subtract(value[i], multiply(ratio[k, i], value[k]))
    weights = [SCALE * jnp.concatenate([v[0], v[0]], axis=0) for v in value]

    pairs = []
    for layer in range(3):
        fields = []
        for comp in range(3):
            total = weights[0] * basis[0, comp, layer]
            for step in range(1, ITERS):
                total = total + weights[step] * basis[step, comp, layer]
            if layer > 0:
                displacement[comp, layer - 1] = total[0:8]
            fields.append(node_pairs(total, last=False))
        pairs.append(fields)
    for layer in range(2):
        u, v, w = element_modes(pairs[layer], pairs[layer + 1])
        strain = (
            0.25 * u["dss"],
            0.25 * v["sds"],
            0.25 * w["ssd"],
            0.125 * (w["sds"] + v["ssd"]),
            0.125 * (w["dss"] + u["ssd"]),
            0.125 * (v["dss"] + u["sds"]),
        )
        index = own[18 + layer].astype(jnp.int32) + CLASSES
        entries = jnp.broadcast_to(table[3:4], (8, 128))
        retain = jnp.take_along_axis(entries, index, axis=1, mode="promise_in_bounds")
        for part in range(6):
            old = own[6 + 2 * part + layer]
            viscous_next[part, layer] = retain * old + (1.0 - retain) * strain[part][0:8]


def shifted(value, axes, count, steps):
    pairs = [(i, i + steps) for i in range(count) if 0 <= i + steps < count]
    return lax.ppermute(value, axes, pairs)


def solution(mesh):
    count_x, count_z = mesh.shape["gx"], mesh.shape["gy"]
    along = min(8, count_x // 2)
    across = count_x // (2 * along)
    grid = Mesh(mesh.devices.reshape(across, along, 2, count_z), ("y", "x", "core", "z"))
    chips = along * across

    def shards(load, viscous, material, free_nodes, moduli_table, relax_time):
        own, low, high, table = call(
            pack_body,
            (SDS((22, 8, 128), F32), SDS((11, 8, 128), F32), SDS((11, 8, 128), F32), SDS((8, 128), F32)),
            6,
            scratch=(
                pltpu.VMEM((2, 8, 128), jnp.int32),
                pltpu.VMEM((2, 8, 128), jnp.int32),
                pltpu.VMEM((3, CLASSES), F32),
                pltpu.VMEM((1, CLASSES), F32),
                pltpu.SemaphoreType.DMA((6,)),
            ),
            first=HBM,
        )(
            *(
                pltpu.with_memory_space_constraint(value, pltpu.HBM)
                for value in (
                    load.reshape(6, 8, 128),
                    viscous.reshape(12, 8, 128),
                    material,
                    free_nodes,
                    moduli_table,
                    relax_time.reshape(1, CLASSES),
                )
            )
        )
        below = shifted(high, ("z",), count_z, 1)
        above = shifted(low, ("z",), count_z, -1)
        wide = call(widen_body, SDS((BLOCK, ROWS, 128), F32), 4)(own, above, below, table)
        left = shifted(wide, ("y", "x"), chips, 1)
        right = shifted(wide, ("y", "x"), chips, -1)
        core = lax.axis_index("core").astype(jnp.int32).reshape(1)
        given = call(choose_body, SDS((2, BLOCK, ROWS, 128), F32), 4, first=SMEM)(core, wide, left, right)
        taken = lax.ppermute(given, ("core",), [(0, 1), (1, 0)])
        near, far = 2 * along, across * count_z
        basis, sums = call(
            krylov_body,
            (SDS((ITERS, 3, 3, ROWS, 128), F32), SDS((near, 128), F32)),
            5,
            scratch=(
                pltpu.VMEM((ITERS, 3, LAYERS, ROWS, 128), F32),
                pltpu.VMEM((LAYERS, ROWS, 128), F32),
                pltpu.VMEM((5, LAYERS, ROWS, 128), F32),
            ),
            flops=20000000,
        )(left, taken, wide, right, table)
        group = lax.all_to_all(sums.reshape(near, 1, 128), ("x", "core"), 0, 0)
        partial = call(middle_body, SDS((far, 128), F32), 1)(group.reshape(near, 128))
        everything = lax.all_to_all(partial.reshape(far, 1, 128), ("y", "z"), 0, 0)
        return tuple(
            call(final_body, (SDS((3, 2, 8, 128), F32), SDS((6, 2, 8, 128), F32)), 4)(
                jnp.pad(everything.reshape(far, 128), ((0, -far % 8), (0, 0))), basis, own, table
            )
        )

    return jax.shard_map(
        shards,
        mesh=grid,
        in_specs=(
            P(None, ("y", "x", "core"), "z", None),
            P(None, ("y", "x", "core"), "z", None),
            P(("y", "x", "core"), "z", None),
            P(("y", "x", "core"), "z", None),
            P(),
            P(),
        ),
        out_specs=(P(None, ("y", "x", "core"), "z", None), P(None, ("y", "x", "core"), "z", None)),
        check_vma=False,
    )
```

```python
import math

import jax
import jax.numpy as jnp
from jax import lax
from jax.experimental import pallas as pl
from jax.experimental.pallas import tpu as pltpu
from jax.sharding import Mesh, PartitionSpec as P

ITERS = 4
ROWS = 16
LAYERS = 10
FIELDS = 11
BLOCK = 13
CLASSES = 16
MOMENTS = 2 * ITERS
SCALE = 1.0 / 32.0
TINY_PIVOT = 1e-9

F32 = jnp.float32
SDS = jax.ShapeDtypeStruct
VMEM = pl.BlockSpec(memory_space=pltpu.VMEM)
SMEM = pl.BlockSpec(memory_space=pltpu.SMEM)
HBM = pl.BlockSpec(memory_space=pltpu.HBM)
PAIRS = ("ss", "sd", "ds", "dd")


def call(body, out_shape, n_in, scratch=(), spec=VMEM, scalars=0, flops=100000):
    many = isinstance(out_shape, (list, tuple))
    return pl.pallas_call(
        body,
        out_shape=out_shape,
        in_specs=[SMEM] * scalars + [spec] * (n_in - scalars),
        out_specs=[VMEM] * len(out_shape) if many else VMEM,
        scratch_shapes=list(scratch),
        compiler_params=pltpu.CompilerParams(vmem_limit_bytes=24 * 1024 * 1024),
        cost_estimate=pl.CostEstimate(flops=flops, bytes_accessed=100000, transcendentals=0),
    )


def pack_body(
    odd, load, viscous, material, free, moduli, relax, own, first, second, table, kinds, frees, entries, times, done
):
    pairs = (
        (load, own.at[0:6]),
        (viscous, own.at[6:18]),
        (material, kinds),
        (free, frees),
        (moduli, entries),
        (relax, times),
    )
    copies = [pltpu.make_async_copy(source, target, done.at[k]) for k, (source, target) in enumerate(pairs)]
    for copy in copies:
        copy.start()
    for copy in copies:
        copy.wait()
    row = lax.broadcasted_iota(jnp.int32, (8, 128), 0)
    even = jnp.full((8, 128), odd[0], jnp.int32) == 0
    for field in range(FIELDS):
        if field == 9:
            layers = [kinds[layer].astype(F32) - float(CLASSES) for layer in range(2)]
        elif field == 10:
            layers = [frees[layer].astype(F32) for layer in range(2)]
        else:
            layers = [own[2 * field + layer] for layer in range(2)]
        if field >= 9:
            for layer in range(2):
                own[2 * field + layer] = layers[layer]
        low = jnp.where(row < 4, layers[0], pltpu.roll(layers[1], 4, 0))
        high = jnp.where(row < 4, pltpu.roll(layers[0], 4, 0), layers[1])
        first[field] = jnp.where(even, high, low)
        second[field] = jnp.where(even, low, high)
    time = times[...]
    retain = time / (time + 1.0)
    table[...] = jnp.zeros((8, 128), F32)
    table[0:1, 0:CLASSES] = entries[0:1] * (1.0 / 16.0)
    table[1:2, 0:CLASSES] = entries[1:2] * (1.0 / 16.0)
    table[2:3, 0:CLASSES] = (entries[2:3] * retain) * (1.0 / 16.0)
    table[3:4, 0:CLASSES] = retain


def pick(table, row, index):
    entries = jnp.broadcast_to(table[row : row + 1], index.shape)
    return jnp.take_along_axis(entries, index, axis=1, mode="promise_in_bounds")


def widen_body(odd, own, first, second, table, wide):
    row = lax.broadcasted_iota(jnp.int32, (8, 128), 0)
    even = jnp.full((8, 128), odd[0], jnp.int32) == 0

    def rows(field):
        upper = jnp.where(even, first[field], second[field])
        lower = jnp.where(even, second[field], first[field])
        halos = (
            jnp.where(row < 4, upper, pltpu.roll(lower, 4, 0)),
            jnp.where(row < 4, pltpu.roll(upper, 4, 0), lower),
        )
        return [jnp.concatenate([own[2 * field + layer], halos[layer]], axis=0) for layer in range(2)]

    fields = [rows(field) for field in range(FIELDS)]
    for layer in range(2):
        wide[9 + layer] = fields[9][layer]
        wide[11 + layer] = fields[10][layer]
    pending = None
    for layer in range(2):
        index = fields[9][layer].astype(jnp.int32) + CLASSES
        factor = 8.0 * pick(table, 2, index)
        xx, yy, zz, yz, xz, xy = (factor * fields[3 + part][layer] for part in range(6))
        forces = (
            {"dss": xx, "ssd": xz, "sds": xy},
            {"sds": yy, "ssd": yz, "dss": xy},
            {"ssd": zz, "sds": yz, "dss": xz},
        )
        upper, lower = to_nodes(forces)
        pairs = lower if pending is None else merged(pending, lower)
        for comp in range(3):
            force = node_force(pairs[comp])
            wide[3 * comp + layer] = force if layer == 0 else fields[comp][0] + force
        pending = upper
    for comp in range(3):
        wide[3 * comp + 2] = fields[comp][1] + node_force(pending[comp])


def choose_body(core, odd, wide, first, second, given, sides):
    @pl.when(odd[0] == 0)
    def _():
        sides[0] = second[...]
        sides[1] = first[...]

    @pl.when(odd[0] != 0)
    def _():
        sides[0] = first[...]
        sides[1] = second[...]

    @pl.when(core[0] == 0)
    def _():
        given[0] = wide[...]
        given[1] = sides[1]

    @pl.when(core[0] != 0)
    def _():
        given[0] = sides[0]
        given[1] = wide[...]


def iota(axis, shape=(ROWS, 128)):
    return lax.broadcasted_iota(jnp.int32, shape, axis)


def next_lane(tile):
    return jnp.where(iota(1) < 127, pltpu.roll(tile, 127, 1), 0.0)


def previous_lane(tile):
    return jnp.where(iota(1) > 0, pltpu.roll(tile, 1, 1), 0.0)


def node_pairs(tile, last=True):
    lower = pltpu.roll(tile, 1, 0)
    parts = {}
    for name, part in (("s", tile + lower), ("d", tile - lower)):
        upper = next_lane(part)
        parts[name + "s"] = part + upper
        if last or name == "s":
            parts[name + "d"] = upper - part
    return parts


def element_modes(lower, upper):
    modes = []
    for below, above in zip(lower, upper):
        mode = {"d" + pair: above[pair] - below[pair] for pair in above}
        mode.update({"s" + pair: above[pair] + below[pair] for pair in above if pair != "ss"})
        modes.append(mode)
    return modes


def element_loads(modes, moduli):
    lame, both, lame_third, shear_third, cubic = moduli
    u, v, w = modes
    fu, fv, fw = {}, {}, {}
    trace = lame * (u["dss"] + v["sds"] + w["ssd"])
    twice = both + both
    fu["dss"] = trace + twice * u["dss"]
    fv["sds"] = trace + twice * v["sds"]
    fw["ssd"] = trace + twice * w["ssd"]
    fw["sds"] = fv["ssd"] = both * (w["sds"] + v["ssd"])
    fw["dss"] = fu["ssd"] = both * (w["dss"] + u["ssd"])
    fv["dss"] = fu["sds"] = both * (v["dss"] + u["sds"])
    triple = 3.0 * shear_third
    part = lame_third * (u["dds"] + w["sdd"])
    fu["dds"] = part + triple * u["dds"]
    fw["sdd"] = part + triple * w["sdd"]
    part = lame_third * (v["dds"] + w["dsd"])
    fv["dds"] = part + triple * v["dds"]
    fw["dsd"] = part + triple * w["dsd"]
    part = lame_third * (u["dsd"] + v["sdd"])
    fu["dsd"] = part + triple * u["dsd"]
    fv["sdd"] = part + triple * v["sdd"]
    part = w["dds"] + v["dsd"] + u["sdd"]
    fw["dds"] = shear_third * (part + w["dds"])
    fv["dsd"] = shear_third * (part + v["dsd"])
    fu["sdd"] = shear_third * (part + u["sdd"])
    for mode, force in zip(modes, (fu, fv, fw)):
        force["ddd"] = cubic * mode["ddd"]
    return fu, fv, fw


def plus(a, b):
    return b if a is None else a if b is None else a + b


def to_nodes(forces):
    uppers, lowers = [], []
    for force in forces:
        upper, lower = {}, {}
        for pair in PAIRS:
            s, d = force.get("s" + pair), force.get("d" + pair)
            upper[pair] = plus(s, d)
            lower[pair] = None if s is None and d is None else (-d if s is None else s if d is None else s - d)
        uppers.append(upper)
        lowers.append(lower)
    return uppers, lowers


def node_force(pairs):
    along = {}
    for name in "sd":
        s, d = pairs[name + "s"], pairs[name + "d"]
        if d is None:
            along[name] = s + previous_lane(s)
        else:
            along[name] = (s - d) + previous_lane(s + d)
    return (along["s"] + along["d"]) + pltpu.roll(along["s"] - along["d"], ROWS - 1, 0)


def merged(first, second):
    return [{pair: plus(a[pair], b[pair]) for pair in PAIRS} for a, b in zip(first, second)]


def krylov_body(sides, rec, wide, table, basis, sums, vec, mask, moduli):
    blocks = (sides.at[0], rec.at[0], wide, rec.at[1], sides.at[1])
    for layer in range(LAYERS):
        block, place = blocks[layer // 2], layer % 2
        index = block[9 + place].astype(jnp.int32) + CLASSES
        lame, shear, arm = (pick(table, row, index) for row in range(3))
        moduli[0, layer] = lame
        moduli[1, layer] = shear + arm
        moduli[2, layer] = lame * (1.0 / 3.0)
        moduli[3, layer] = shear * (1.0 / 3.0)
        moduli[4, layer] = (lame + 4.0 * shear) * (1.0 / 9.0)
        mask[layer] = block[11 + place]
        if layer < LAYERS - 1:
            for comp in range(3):
                force = block[3 * comp + 1 + place]
                if place == 1:
                    force = force + blocks[layer // 2 + 1][3 * comp]
                vec[0, comp, layer] = mask[layer] * force

    def masked_pairs(step, layer):
        return [node_pairs(mask[layer] * vec[step, comp, layer]) for comp in range(3)]

    for step in range(ITERS - 1):
        below = masked_pairs(step, step)
        pending = None
        for layer in range(step + 1, LAYERS - 1 - step):
            above = masked_pairs(step, layer)
            loads = element_loads(element_modes(below, above), [moduli[k, layer] for k in range(5)])
            upper, lower = to_nodes(loads)
            if pending is not None:
                node = layer - 1
                free = mask[node]
                for comp, pairs in enumerate(merged(pending, lower)):
                    value = vec[step, comp, node]
                    image = free * node_force(pairs) + (1.0 - free) * value
                    vec[step + 1, comp, node] = SCALE * image
            pending = upper
            below = above

    last = ITERS - 1
    energy = jnp.zeros((8, 128), F32)
    below = masked_pairs(last, 3)
    for layer in (4, 5):
        above = masked_pairs(last, layer)
        modes = element_modes(below, above)
        loads = element_loads(modes, [moduli[k, layer] for k in range(5)])
        total = None
        for mode, force in zip(modes, loads):
            for name in force:
                total = plus(total, (mode[name] * force[name])[0:8])
        energy = energy + total
        for comp in range(3):
            value = vec[last, comp, layer, 0:8]
            energy = energy + (1.0 - mask[layer, 0:8]) * value * value
        below = above

    moments = []
    for k in range(MOMENTS - 1):
        total = None
        for comp in range(3):
            for layer in (4, 5):
                total = plus(total, vec[k // 2, comp, layer, 0:8] * vec[(k + 1) // 2, comp, layer, 0:8])
        moments.append(total)
    moments.append(SCALE * energy)
    row, lane = iota(0, (8, 128)), iota(1, (8, 128))
    rows = jnp.zeros((8, 128), F32)
    for k, total in enumerate(moments):
        rows = jnp.where(row == k, jnp.sum(total, axis=0, keepdims=True), rows)
    for step in (64, 32, 16):
        rows = rows + pltpu.roll(rows, step, 1)
    line = jnp.sum(jnp.where(lane // 16 == row, rows, 0.0), axis=0, keepdims=True)
    sums[...] = jnp.broadcast_to(line, sums.shape)
    for step in range(ITERS):
        for comp in range(3):
            for layer in range(3):
                basis[step, comp, layer] = vec[step, comp, 3 + layer]


def two_sum(a, b):
    total = a + b
    part = total - a
    return total, (a - (total - part)) + (b - part)


def settle(high, low):
    total = high + low
    return total, low - (total - high)


def add(a, b):
    total, rest = two_sum(a[0], b[0])
    return settle(total, rest + (a[1] + b[1]))


def halves(a):
    wide = 4097.0 * a
    high = wide - (wide - a)
    return high, a - high


def two_product(a, b):
    total = a * b
    (ah, al), (bh, bl) = halves(a), halves(b)
    return total, ((ah * bh - total) + ah * bl + al * bh) + al * bl


def multiply(a, b):
    total, rest = two_product(a[0], b[0])
    return settle(total, rest + (a[0] * b[1] + a[1] * b[0]))


def subtract(a, b):
    return add(a, (-b[0], -b[1]))


def invert(a):
    first = 1.0 / a[0]
    total, rest = two_product(a[0], first)
    return settle(first, first * (((1.0 - total) - rest) - a[1] * first))


def rolled(a, steps, axis):
    return tuple(pltpu.roll(part, steps, axis) for part in a)


def over_rows(pair):
    for step in (4, 2, 1):
        pair = add(pair, rolled(pair, step, 0))
    return pair


def total_of(pairs):
    while len(pairs) > 1:
        pairs = [add(*pairs[k : k + 2]) if k + 1 < len(pairs) else pairs[k] for k in range(0, len(pairs), 2)]
    return pairs[0]


def middle_body(sums, out):
    pair = over_rows(total_of([(sums[k : k + 8], jnp.zeros((8, 128), F32)) for k in range(0, sums.shape[0], 8)]))
    high, low = add(pair, rolled(pair, 120, 1))
    line = jnp.where(iota(1, (8, 128)) % 16 < 8, high, pltpu.roll(low, 8, 1))
    for k in range(0, out.shape[0], 8):
        count = min(8, out.shape[0] - k)
        out[k : k + count] = line[0:count]


def final_body(sums, basis, own, table, displacement, viscous_next):
    pairs = []
    for k in range(sums.shape[0] // 8):
        tile = sums[8 * k : 8 * k + 8]
        pairs.append((tile, pltpu.roll(tile, 120, 1)))
    pair = over_rows(total_of(pairs))
    for step in (4, 2, 1):
        pair = add(pair, rolled(pair, 128 - step, 1))

    def moment(k):
        index = jnp.full((8, 128), 16 * k, jnp.int32)
        return tuple(jnp.take_along_axis(part, index, axis=1, mode="promise_in_bounds") for part in pair)

    moments = [moment(k) for k in range(MOMENTS)]
    matrix = [[moments[i + j + 1] for j in range(i + 1)] for i in range(ITERS)]
    value = moments[:ITERS]
    ratio = {}
    inverse = []
    for k in range(ITERS):
        pivot = matrix[k][k]
        kept = pivot[0] > TINY_PIVOT * moments[2 * k + 1][0]
        inverse.append(tuple(jnp.where(kept, part, 0.0) for part in invert(pivot)))
        for i in range(k + 1, ITERS):
            ratio[i, k] = multiply(matrix[i][k], inverse[k])
            for j in range(k + 1, i + 1):
                matrix[i][j] = subtract(matrix[i][j], multiply(ratio[i, k], matrix[j][k]))
            value[i] = subtract(value[i], multiply(ratio[i, k], value[k]))
    value = [multiply(value[k], inverse[k]) for k in range(ITERS)]
    for k in reversed(range(ITERS)):
        for i in range(k):
            value[i] = subtract(value[i], multiply(ratio[k, i], value[k]))
    weights = [SCALE * jnp.concatenate([v[0], v[0]], axis=0) for v in value]

    pairs = []
    for layer in range(3):
        fields = []
        for comp in range(3):
            total = weights[0] * basis[0, comp, layer]
            for step in range(1, ITERS):
                total = total + weights[step] * basis[step, comp, layer]
            if layer > 0:
                displacement[comp, layer - 1] = total[0:8]
            fields.append(node_pairs(total, last=False))
        pairs.append(fields)
    for layer in range(2):
        u, v, w = element_modes(pairs[layer], pairs[layer + 1])
        strain = (
            0.25 * u["dss"],
            0.25 * v["sds"],
            0.25 * w["ssd"],
            0.125 * (w["sds"] + v["ssd"]),
            0.125 * (w["dss"] + u["ssd"]),
            0.125 * (v["dss"] + u["sds"]),
        )
        index = own[18 + layer].astype(jnp.int32) + CLASSES
        entries = jnp.broadcast_to(table[3:4], (8, 128))
        retain = jnp.take_along_axis(entries, index, axis=1, mode="promise_in_bounds")
        for part in range(6):
            old = own[6 + 2 * part + layer]
            viscous_next[part, layer] = retain * old + (1.0 - retain) * strain[part][0:8]


def swapped(value, axes, count, start):
    lower = [i for i in range(start, count - 1, 2)]
    return lax.ppermute(value, axes, [(i, i + 1) for i in lower] + [(i + 1, i) for i in lower])


def solution(mesh):
    count_x, count_z = mesh.shape["gx"], mesh.shape["gy"]
    along = min(8, count_x // 2)
    across = count_x // (2 * along)
    grid = Mesh(mesh.devices.reshape(across, along, 2, count_z), ("y", "x", "core", "z"))
    chips = along * across

    def shards(load, viscous, material, free_nodes, moduli_table, relax_time):
        def parity(axes):
            return (lax.axis_index(axes) % 2).astype(jnp.int32).reshape(1)

        odd_row, odd_chip, core = parity("z"), parity("x"), parity("core")
        own, first, second, table = call(
            pack_body,
            (SDS((22, 8, 128), F32), SDS((11, 8, 128), F32), SDS((11, 8, 128), F32), SDS((8, 128), F32)),
            7,
            scratch=(
                pltpu.VMEM((2, 8, 128), jnp.int32),
                pltpu.VMEM((2, 8, 128), jnp.int32),
                pltpu.VMEM((3, CLASSES), F32),
                pltpu.VMEM((1, CLASSES), F32),
                pltpu.SemaphoreType.DMA((6,)),
            ),
            spec=HBM,
            scalars=1,
        )(
            odd_row,
            *(
                pltpu.with_memory_space_constraint(value, pltpu.HBM)
                for value in (
                    load.reshape(6, 8, 128),
                    viscous.reshape(12, 8, 128),
                    material,
                    free_nodes,
                    moduli_table,
                    relax_time.reshape(1, CLASSES),
                )
            )
        )
        first = swapped(first, ("z",), count_z, 0)
        second = swapped(second, ("z",), count_z, 1)
        wide = call(widen_body, SDS((BLOCK, ROWS, 128), F32), 5, scalars=1)(odd_row, own, first, second, table)
        first = swapped(wide, ("y", "x"), chips, 0)
        second = swapped(wide, ("y", "x"), chips, 1)
        given, sides = call(
            choose_body,
            (SDS((2, BLOCK, ROWS, 128), F32), SDS((2, BLOCK, ROWS, 128), F32)),
            5,
            scalars=2,
        )(core, odd_chip, wide, first, second)
        taken = lax.ppermute(given, ("core",), [(0, 1), (1, 0)])
        near, far = 2 * along, across * count_z
        basis, sums = call(
            krylov_body,
            (SDS((ITERS, 3, 3, ROWS, 128), F32), SDS((near, 128), F32)),
            4,
            scratch=(
                pltpu.VMEM((ITERS, 3, LAYERS, ROWS, 128), F32),
                pltpu.VMEM((LAYERS, ROWS, 128), F32),
                pltpu.VMEM((5, LAYERS, ROWS, 128), F32),
            ),
            flops=20000000,
        )(sides, taken, wide, table)
        group = lax.all_to_all(sums.reshape(near, 1, 128), ("x", "core"), 0, 0)
        partial = call(middle_body, SDS((far, 128), F32), 1)(group.reshape(near, 128))
        everything = lax.all_to_all(partial.reshape(far, 1, 128), ("y", "z"), 0, 0)
        return tuple(
            call(final_body, (SDS((3, 2, 8, 128), F32), SDS((6, 2, 8, 128), F32)), 4)(
                jnp.pad(everything.reshape(far, 128), ((0, -far % 8), (0, 0))), basis, own, table
            )
        )

    return jax.shard_map(
        shards,
        mesh=grid,
        in_specs=(
            P(None, ("y", "x", "core"), "z", None),
            P(None, ("y", "x", "core"), "z", None),
            P(("y", "x", "core"), "z", None),
            P(("y", "x", "core"), "z", None),
            P(),
            P(),
        ),
        out_specs=(P(None, ("y", "x", "core"), "z", None), P(None, ("y", "x", "core"), "z", None)),
        check_vma=False,
    )
```

```python
import math

import jax
import jax.numpy as jnp
from jax import lax
from jax.experimental import pallas as pl
from jax.experimental.pallas import tpu as pltpu
from jax.sharding import Mesh, PartitionSpec as P

ITERS = 4
ROWS = 16
LAYERS = 10
FIELDS = 11
BLOCK = 13
CLASSES = 16
MOMENTS = 2 * ITERS
SCALE = 1.0 / 32.0
TINY_PIVOT = 1e-9

F32 = jnp.float32
SDS = jax.ShapeDtypeStruct
VMEM = pl.BlockSpec(memory_space=pltpu.VMEM)
SMEM = pl.BlockSpec(memory_space=pltpu.SMEM)
HBM = pl.BlockSpec(memory_space=pltpu.HBM)
PAIRS = ("ss", "sd", "ds", "dd")


def call(body, out_shape, n_in, scratch=(), spec=VMEM, scalars=0, flops=100000):
    many = isinstance(out_shape, (list, tuple))
    return pl.pallas_call(
        body,
        out_shape=out_shape,
        in_specs=[SMEM] * scalars + [spec] * (n_in - scalars),
        out_specs=[VMEM] * len(out_shape) if many else VMEM,
        scratch_shapes=list(scratch),
        compiler_params=pltpu.CompilerParams(vmem_limit_bytes=24 * 1024 * 1024),
        cost_estimate=pl.CostEstimate(flops=flops, bytes_accessed=100000, transcendentals=0),
    )


def pack_body(load, viscous, material, free, moduli, relax, own, low, high, table, kinds, frees, entries, times, done):
    pairs = (
        (load, own.at[0:6]),
        (viscous, own.at[6:18]),
        (material, kinds),
        (free, frees),
        (moduli, entries),
        (relax, times),
    )
    copies = [pltpu.make_async_copy(source, target, done.at[k]) for k, (source, target) in enumerate(pairs)]
    for copy in copies:
        copy.start()
    for copy in copies:
        copy.wait()
    row = lax.broadcasted_iota(jnp.int32, (8, 128), 0)
    for field in range(FIELDS):
        if field == 9:
            layers = [kinds[layer].astype(F32) - float(CLASSES) for layer in range(2)]
        elif field == 10:
            layers = [frees[layer].astype(F32) for layer in range(2)]
        else:
            layers = [own[2 * field + layer] for layer in range(2)]
        if field >= 9:
            for layer in range(2):
                own[2 * field + layer] = layers[layer]
        low[field] = jnp.where(row < 4, layers[0], pltpu.roll(layers[1], 4, 0))
        high[field] = jnp.where(row < 4, pltpu.roll(layers[0], 4, 0), layers[1])
    time = times[...]
    retain = time / (time + 1.0)
    table[...] = jnp.zeros((8, 128), F32)
    table[0:1, 0:CLASSES] = entries[0:1] * (1.0 / 16.0)
    table[1:2, 0:CLASSES] = entries[1:2] * (1.0 / 16.0)
    table[2:3, 0:CLASSES] = (entries[2:3] * retain) * (1.0 / 16.0)
    table[3:4, 0:CLASSES] = retain


def pick(table, row, index):
    entries = jnp.broadcast_to(table[row : row + 1], index.shape)
    return jnp.take_along_axis(entries, index, axis=1, mode="promise_in_bounds")


def widen_body(own, above, below, table, wide):
    row = lax.broadcasted_iota(jnp.int32, (8, 128), 0)

    def rows(field):
        upper, lower = above[field], below[field]
        halos = (
            jnp.where(row < 4, upper, pltpu.roll(lower, 4, 0)),
            jnp.where(row < 4, pltpu.roll(upper, 4, 0), lower),
        )
        return [jnp.concatenate([own[2 * field + layer], halos[layer]], axis=0) for layer in range(2)]

    fields = [rows(field) for field in range(FIELDS)]
    for layer in range(2):
        wide[9 + layer] = fields[9][layer]
        wide[11 + layer] = fields[10][layer]
    pending = None
    for layer in range(2):
        index = fields[9][layer].astype(jnp.int32) + CLASSES
        factor = 8.0 * pick(table, 2, index)
        xx, yy, zz, yz, xz, xy = (factor * fields[3 + part][layer] for part in range(6))
        forces = (
            {"dss": xx, "ssd": xz, "sds": xy},
            {"sds": yy, "ssd": yz, "dss": xy},
            {"ssd": zz, "sds": yz, "dss": xz},
        )
        upper, lower = to_nodes(forces)
        pairs = lower if pending is None else merged(pending, lower)
        for comp in range(3):
            force = node_force(pairs[comp])
            wide[3 * comp + layer] = force if layer == 0 else fields[comp][0] + force
        pending = upper
    for comp in range(3):
        wide[3 * comp + 2] = fields[comp][1] + node_force(pending[comp])


def choose_body(core, odd, wide, first, second, given, sides):
    @pl.when(odd[0] == 0)
    def _():
        sides[0] = second[...]
        sides[1] = first[...]

    @pl.when(odd[0] != 0)
    def _():
        sides[0] = first[...]
        sides[1] = second[...]

    @pl.when(core[0] == 0)
    def _():
        given[0] = wide[...]
        given[1] = sides[1]

    @pl.when(core[0] != 0)
    def _():
        given[0] = sides[0]
        given[1] = wide[...]


def iota(axis, shape=(ROWS, 128)):
    return lax.broadcasted_iota(jnp.int32, shape, axis)


def next_lane(tile):
    return jnp.where(iota(1) < 127, pltpu.roll(tile, 127, 1), 0.0)


def previous_lane(tile):
    return jnp.where(iota(1) > 0, pltpu.roll(tile, 1, 1), 0.0)


def node_pairs(tile, last=True):
    lower = pltpu.roll(tile, 1, 0)
    parts = {}
    for name, part in (("s", tile + lower), ("d", tile - lower)):
        upper = next_lane(part)
        parts[name + "s"] = part + upper
        if last or name == "s":
            parts[name + "d"] = upper - part
    return parts


def element_modes(lower, upper):
    modes = []
    for below, above in zip(lower, upper):
        mode = {"d" + pair: above[pair] - below[pair] for pair in above}
        mode.update({"s" + pair: above[pair] + below[pair] for pair in above if pair != "ss"})
        modes.append(mode)
    return modes


def element_loads(modes, moduli):
    lame, both, lame_third, shear_third, cubic = moduli
    u, v, w = modes
    fu, fv, fw = {}, {}, {}
    trace = lame * (u["dss"] + v["sds"] + w["ssd"])
    twice = both + both
    fu["dss"] = trace + twice * u["dss"]
    fv["sds"] = trace + twice * v["sds"]
    fw["ssd"] = trace + twice * w["ssd"]
    fw["sds"] = fv["ssd"] = both * (w["sds"] + v["ssd"])
    fw["dss"] = fu["ssd"] = both * (w["dss"] + u["ssd"])
    fv["dss"] = fu["sds"] = both * (v["dss"] + u["sds"])
    triple = 3.0 * shear_third
    part = lame_third * (u["dds"] + w["sdd"])
    fu["dds"] = part + triple * u["dds"]
    fw["sdd"] = part + triple * w["sdd"]
    part = lame_third * (v["dds"] + w["dsd"])
    fv["dds"] = part + triple * v["dds"]
    fw["dsd"] = part + triple * w["dsd"]
    part = lame_third * (u["dsd"] + v["sdd"])
    fu["dsd"] = part + triple * u["dsd"]
    fv["sdd"] = part + triple * v["sdd"]
    part = w["dds"] + v["dsd"] + u["sdd"]
    fw["dds"] = shear_third * (part + w["dds"])
    fv["dsd"] = shear_third * (part + v["dsd"])
    fu["sdd"] = shear_third * (part + u["sdd"])
    for mode, force in zip(modes, (fu, fv, fw)):
        force["ddd"] = cubic * mode["ddd"]
    return fu, fv, fw


def plus(a, b):
    return b if a is None else a if b is None else a + b


def to_nodes(forces):
    uppers, lowers = [], []
    for force in forces:
        upper, lower = {}, {}
        for pair in PAIRS:
            s, d = force.get("s" + pair), force.get("d" + pair)
            upper[pair] = plus(s, d)
            lower[pair] = None if s is None and d is None else (-d if s is None else s if d is None else s - d)
        uppers.append(upper)
        lowers.append(lower)
    return uppers, lowers


def node_force(pairs):
    along = {}
    for name in "sd":
        s, d = pairs[name + "s"], pairs[name + "d"]
        if d is None:
            along[name] = s + previous_lane(s)
        else:
            along[name] = (s - d) + previous_lane(s + d)
    return (along["s"] + along["d"]) + pltpu.roll(along["s"] - along["d"], ROWS - 1, 0)


def merged(first, second):
    return [{pair: plus(a[pair], b[pair]) for pair in PAIRS} for a, b in zip(first, second)]


def krylov_body(sides, rec, wide, table, basis, sums, vec, mask, moduli):
    blocks = (sides.at[0], rec.at[0], wide, rec.at[1], sides.at[1])
    for layer in range(LAYERS):
        block, place = blocks[layer // 2], layer % 2
        index = block[9 + place].astype(jnp.int32) + CLASSES
        lame, shear, arm = (pick(table, row, index) for row in range(3))
        moduli[0, layer] = lame
        moduli[1, layer] = shear + arm
        moduli[2, layer] = lame * (1.0 / 3.0)
        moduli[3, layer] = shear * (1.0 / 3.0)
        moduli[4, layer] = (lame + 4.0 * shear) * (1.0 / 9.0)
        mask[layer] = block[11 + place]
        if layer < LAYERS - 1:
            for comp in range(3):
                force = block[3 * comp + 1 + place]
                if place == 1:
                    force = force + blocks[layer // 2 + 1][3 * comp]
                vec[0, comp, layer] = mask[layer] * force

    def masked_pairs(step, layer):
        return [node_pairs(mask[layer] * vec[step, comp, layer]) for comp in range(3)]

    for step in range(ITERS - 1):
        below = masked_pairs(step, step)
        pending = None
        for layer in range(step + 1, LAYERS - 1 - step):
            above = masked_pairs(step, layer)
            loads = element_loads(element_modes(below, above), [moduli[k, layer] for k in range(5)])
            upper, lower = to_nodes(loads)
            if pending is not None:
                node = layer - 1
                free = mask[node]
                for comp, pairs in enumerate(merged(pending, lower)):
                    value = vec[step, comp, node]
                    image = free * node_force(pairs) + (1.0 - free) * value
                    vec[step + 1, comp, node] = SCALE * image
            pending = upper
            below = above

    last = ITERS - 1
    energy = jnp.zeros((8, 128), F32)
    below = masked_pairs(last, 3)
    for layer in (4, 5):
        above = masked_pairs(last, layer)
        modes = element_modes(below, above)
        loads = element_loads(modes, [moduli[k, layer] for k in range(5)])
        total = None
        for mode, force in zip(modes, loads):
            for name in force:
                total = plus(total, (mode[name] * force[name])[0:8])
        energy = energy + total
        for comp in range(3):
            value = vec[last, comp, layer, 0:8]
            energy = energy + (1.0 - mask[layer, 0:8]) * value * value
        below = above

    moments = []
    for k in range(MOMENTS - 1):
        total = None
        for comp in range(3):
            for layer in (4, 5):
                total = plus(total, vec[k // 2, comp, layer, 0:8] * vec[(k + 1) // 2, comp, layer, 0:8])
        moments.append(total)
    moments.append(SCALE * energy)
    row, lane = iota(0, (8, 128)), iota(1, (8, 128))
    rows = jnp.zeros((8, 128), F32)
    for k, total in enumerate(moments):
        rows = jnp.where(row == k, jnp.sum(total, axis=0, keepdims=True), rows)
    for step in (64, 32, 16):
        rows = rows + pltpu.roll(rows, step, 1)
    line = jnp.sum(jnp.where(lane // 16 == row, rows, 0.0), axis=0, keepdims=True)
    sums[...] = jnp.broadcast_to(line, sums.shape)
    for step in range(ITERS):
        for comp in range(3):
            for layer in range(3):
                basis[step, comp, layer] = vec[step, comp, 3 + layer]


def two_sum(a, b):
    total = a + b
    part = total - a
    return total, (a - (total - part)) + (b - part)


def settle(high, low):
    total = high + low
    return total, low - (total - high)


def add(a, b):
    total, rest = two_sum(a[0], b[0])
    return settle(total, rest + (a[1] + b[1]))


def halves(a):
    wide = 4097.0 * a
    high = wide - (wide - a)
    return high, a - high


def two_product(a, b):
    total = a * b
    (ah, al), (bh, bl) = halves(a), halves(b)
    return total, ((ah * bh - total) + ah * bl + al * bh) + al * bl


def multiply(a, b):
    total, rest = two_product(a[0], b[0])
    return settle(total, rest + (a[0] * b[1] + a[1] * b[0]))


def subtract(a, b):
    return add(a, (-b[0], -b[1]))


def invert(a):
    first = 1.0 / a[0]
    total, rest = two_product(a[0], first)
    return settle(first, first * (((1.0 - total) - rest) - a[1] * first))


def rolled(a, steps, axis):
    return tuple(pltpu.roll(part, steps, axis) for part in a)


def over_rows(pair):
    for step in (4, 2, 1):
        pair = add(pair, rolled(pair, step, 0))
    return pair


def total_of(pairs):
    while len(pairs) > 1:
        pairs = [add(*pairs[k : k + 2]) if k + 1 < len(pairs) else pairs[k] for k in range(0, len(pairs), 2)]
    return pairs[0]


def middle_body(sums, out):
    pair = over_rows(total_of([(sums[k : k + 8], jnp.zeros((8, 128), F32)) for k in range(0, sums.shape[0], 8)]))
    high, low = add(pair, rolled(pair, 120, 1))
    line = jnp.where(iota(1, (8, 128)) % 16 < 8, high, pltpu.roll(low, 8, 1))
    for k in range(0, out.shape[0], 8):
        count = min(8, out.shape[0] - k)
        out[k : k + count] = line[0:count]


def final_body(sums, basis, own, table, displacement, viscous_next):
    pairs = []
    for k in range(sums.shape[0] // 8):
        tile = sums[8 * k : 8 * k + 8]
        pairs.append((tile, pltpu.roll(tile, 120, 1)))
    pair = over_rows(total_of(pairs))
    for step in (4, 2, 1):
        pair = add(pair, rolled(pair, 128 - step, 1))

    def moment(k):
        index = jnp.full((8, 128), 16 * k, jnp.int32)
        return tuple(jnp.take_along_axis(part, index, axis=1, mode="promise_in_bounds") for part in pair)

    moments = [moment(k) for k in range(MOMENTS)]
    matrix = [[moments[i + j + 1] for j in range(i + 1)] for i in range(ITERS)]
    value = moments[:ITERS]
    ratio = {}
    inverse = []
    for k in range(ITERS):
        pivot = matrix[k][k]
        kept = pivot[0] > TINY_PIVOT * moments[2 * k + 1][0]
        inverse.append(tuple(jnp.where(kept, part, 0.0) for part in invert(pivot)))
        for i in range(k + 1, ITERS):
            ratio[i, k] = multiply(matrix[i][k], inverse[k])
            for j in range(k + 1, i + 1):
                matrix[i][j] = subtract(matrix[i][j], multiply(ratio[i, k], matrix[j][k]))
            value[i] = subtract(value[i], multiply(ratio[i, k], value[k]))
    value = [multiply(value[k], inverse[k]) for k in range(ITERS)]
    for k in reversed(range(ITERS)):
        for i in range(k):
            value[i] = subtract(value[i], multiply(ratio[k, i], value[k]))
    weights = [SCALE * jnp.concatenate([v[0], v[0]], axis=0) for v in value]

    pairs = []
    for layer in range(3):
        fields = []
        for comp in range(3):
            total = weights[0] * basis[0, comp, layer]
            for step in range(1, ITERS):
                total = total + weights[step] * basis[step, comp, layer]
            if layer > 0:
                displacement[comp, layer - 1] = total[0:8]
            fields.append(node_pairs(total, last=False))
        pairs.append(fields)
    for layer in range(2):
        u, v, w = element_modes(pairs[layer], pairs[layer + 1])
        strain = (
            0.25 * u["dss"],
            0.25 * v["sds"],
            0.25 * w["ssd"],
            0.125 * (w["sds"] + v["ssd"]),
            0.125 * (w["dss"] + u["ssd"]),
            0.125 * (v["dss"] + u["sds"]),
        )
        index = own[18 + layer].astype(jnp.int32) + CLASSES
        entries = jnp.broadcast_to(table[3:4], (8, 128))
        retain = jnp.take_along_axis(entries, index, axis=1, mode="promise_in_bounds")
        for part in range(6):
            old = own[6 + 2 * part + layer]
            viscous_next[part, layer] = retain * old + (1.0 - retain) * strain[part][0:8]


def shifted(value, axes, count, steps):
    pairs = [(i, i + steps) for i in range(count) if 0 <= i + steps < count]
    return lax.ppermute(value, axes, pairs)


def swapped(value, axes, count, start):
    lower = [i for i in range(start, count - 1, 2)]
    return lax.ppermute(value, axes, [(i, i + 1) for i in lower] + [(i + 1, i) for i in lower])


def solution(mesh):
    count_x, count_z = mesh.shape["gx"], mesh.shape["gy"]
    along = min(8, count_x // 2)
    across = count_x // (2 * along)
    grid = Mesh(mesh.devices.reshape(across, along, 2, count_z), ("y", "x", "core", "z"))
    chips = along * across

    def shards(load, viscous, material, free_nodes, moduli_table, relax_time):
        def parity(axes):
            return (lax.axis_index(axes) % 2).astype(jnp.int32).reshape(1)

        odd_chip, core = parity("x"), parity("core")
        own, low, high, table = call(
            pack_body,
            (SDS((22, 8, 128), F32), SDS((11, 8, 128), F32), SDS((11, 8, 128), F32), SDS((8, 128), F32)),
            6,
            scratch=(
                pltpu.VMEM((2, 8, 128), jnp.int32),
                pltpu.VMEM((2, 8, 128), jnp.int32),
                pltpu.VMEM((3, CLASSES), F32),
                pltpu.VMEM((1, CLASSES), F32),
                pltpu.SemaphoreType.DMA((6,)),
            ),
            spec=HBM,
        )(
            *(
                pltpu.with_memory_space_constraint(value, pltpu.HBM)
                for value in (
                    load.reshape(6, 8, 128),
                    viscous.reshape(12, 8, 128),
                    material,
                    free_nodes,
                    moduli_table,
                    relax_time.reshape(1, CLASSES),
                )
            )
        )
        below = shifted(high, ("z",), count_z, 1)
        above = shifted(low, ("z",), count_z, -1)
        wide = call(widen_body, SDS((BLOCK, ROWS, 128), F32), 4)(own, above, below, table)
        first = swapped(wide, ("y", "x"), chips, 0)
        second = swapped(wide, ("y", "x"), chips, 1)
        given, sides = call(
            choose_body,
            (SDS((2, BLOCK, ROWS, 128), F32), SDS((2, BLOCK, ROWS, 128), F32)),
            5,
            scalars=2,
        )(core, odd_chip, wide, first, second)
        taken = lax.ppermute(given, ("core",), [(0, 1), (1, 0)])
        near, far = along * count_z, 2 * across
        basis, sums = call(
            krylov_body,
            (SDS((ITERS, 3, 3, ROWS, 128), F32), SDS((near, 128), F32)),
            4,
            scratch=(
                pltpu.VMEM((ITERS, 3, LAYERS, ROWS, 128), F32),
                pltpu.VMEM((LAYERS, ROWS, 128), F32),
                pltpu.VMEM((5, LAYERS, ROWS, 128), F32),
            ),
            flops=20000000,
        )(sides, taken, wide, table)
        group = lax.all_to_all(sums.reshape(near, 1, 128), ("x", "z"), 0, 0)
        partial = call(middle_body, SDS((far, 128), F32), 1)(group.reshape(near, 128))
        everything = lax.all_to_all(partial.reshape(far, 1, 128), ("y", "core"), 0, 0)
        return tuple(
            call(final_body, (SDS((3, 2, 8, 128), F32), SDS((6, 2, 8, 128), F32)), 4)(
                jnp.pad(everything.reshape(far, 128), ((0, -far % 8), (0, 0))), basis, own, table
            )
        )

    return jax.shard_map(
        shards,
        mesh=grid,
        in_specs=(
            P(None, ("y", "x", "core"), "z", None),
            P(None, ("y", "x", "core"), "z", None),
            P(("y", "x", "core"), "z", None),
            P(("y", "x", "core"), "z", None),
            P(),
            P(),
        ),
        out_specs=(P(None, ("y", "x", "core"), "z", None), P(None, ("y", "x", "core"), "z", None)),
        check_vma=False,
    )
```

```python
import math

import jax
import jax.numpy as jnp
from jax import lax
from jax.experimental import pallas as pl
from jax.experimental.pallas import tpu as pltpu
from jax.sharding import Mesh, PartitionSpec as P

ITERS = 4
ROWS = 16
LAYERS = 10
FIELDS = 11
BLOCK = 13
CLASSES = 16
MOMENTS = 2 * ITERS
SCALE = 1.0 / 32.0
TINY_PIVOT = 1e-9

F32 = jnp.float32
SDS = jax.ShapeDtypeStruct
VMEM = pl.BlockSpec(memory_space=pltpu.VMEM)
SMEM = pl.BlockSpec(memory_space=pltpu.SMEM)
HBM = pl.BlockSpec(memory_space=pltpu.HBM)
PAIRS = ("ss", "sd", "ds", "dd")


def call(body, out_shape, n_in, scratch=(), spec=VMEM, scalars=0, flops=100000):
    many = isinstance(out_shape, (list, tuple))
    return pl.pallas_call(
        body,
        out_shape=out_shape,
        in_specs=[SMEM] * scalars + [spec] * (n_in - scalars),
        out_specs=[VMEM] * len(out_shape) if many else VMEM,
        scratch_shapes=list(scratch),
        compiler_params=pltpu.CompilerParams(vmem_limit_bytes=24 * 1024 * 1024),
        cost_estimate=pl.CostEstimate(flops=flops, bytes_accessed=100000, transcendentals=0),
    )


def pack_body(load, viscous, material, free, moduli, relax, own, low, high, table, kinds, frees, entries, times, done):
    pairs = (
        (load, own.at[0:6]),
        (viscous, own.at[6:18]),
        (material, kinds),
        (free, frees),
        (moduli, entries),
        (relax, times),
    )
    copies = [pltpu.make_async_copy(source, target, done.at[k]) for k, (source, target) in enumerate(pairs)]
    for copy in copies:
        copy.start()
    for copy in copies:
        copy.wait()
    row = lax.broadcasted_iota(jnp.int32, (8, 128), 0)
    for field in range(FIELDS):
        if field == 9:
            layers = [kinds[layer].astype(F32) - float(CLASSES) for layer in range(2)]
        elif field == 10:
            layers = [frees[layer].astype(F32) for layer in range(2)]
        else:
            layers = [own[2 * field + layer] for layer in range(2)]
        if field >= 9:
            for layer in range(2):
                own[2 * field + layer] = layers[layer]
        low[field] = jnp.where(row < 4, layers[0], pltpu.roll(layers[1], 4, 0))
        high[field] = jnp.where(row < 4, pltpu.roll(layers[0], 4, 0), layers[1])
    time = times[...]
    retain = time / (time + 1.0)
    table[...] = jnp.zeros((8, 128), F32)
    table[0:1, 0:CLASSES] = entries[0:1] * (1.0 / 16.0)
    table[1:2, 0:CLASSES] = entries[1:2] * (1.0 / 16.0)
    table[2:3, 0:CLASSES] = (entries[2:3] * retain) * (1.0 / 16.0)
    table[3:4, 0:CLASSES] = retain


def pick(table, row, index):
    entries = jnp.broadcast_to(table[row : row + 1], index.shape)
    return jnp.take_along_axis(entries, index, axis=1, mode="promise_in_bounds")


def widen_body(own, above, below, table, wide):
    row = lax.broadcasted_iota(jnp.int32, (8, 128), 0)

    def rows(field):
        upper, lower = above[field], below[field]
        halos = (
            jnp.where(row < 4, upper, pltpu.roll(lower, 4, 0)),
            jnp.where(row < 4, pltpu.roll(upper, 4, 0), lower),
        )
        return [jnp.concatenate([own[2 * field + layer], halos[layer]], axis=0) for layer in range(2)]

    fields = [rows(field) for field in range(FIELDS)]
    for layer in range(2):
        wide[9 + layer] = fields[9][layer]
        wide[11 + layer] = fields[10][layer]
    pending = None
    for layer in range(2):
        index = fields[9][layer].astype(jnp.int32) + CLASSES
        factor = 8.0 * pick(table, 2, index)
        xx, yy, zz, yz, xz, xy = (factor * fields[3 + part][layer] for part in range(6))
        forces = (
            {"dss": xx, "ssd": xz, "sds": xy},
            {"sds": yy, "ssd": yz, "dss": xy},
            {"ssd": zz, "sds": yz, "dss": xz},
        )
        upper, lower = to_nodes(forces)
        pairs = lower if pending is None else merged(pending, lower)
        for comp in range(3):
            force = node_force(pairs[comp])
            wide[3 * comp + layer] = force if layer == 0 else fields[comp][0] + force
        pending = upper
    for comp in range(3):
        wide[3 * comp + 2] = fields[comp][1] + node_force(pending[comp])


def order_body(core, odd, chip_first, chip_second, own_chip, next_chip, sides, rec):
    @pl.when(odd[0] == 0)
    def _():
        sides[0] = chip_second[...]
        sides[1] = chip_first[...]

    @pl.when(odd[0] != 0)
    def _():
        sides[0] = chip_first[...]
        sides[1] = chip_second[...]

    @pl.when(core[0] == 0)
    def _():
        rec[0] = next_chip[...]
        rec[1] = own_chip[...]

    @pl.when(core[0] != 0)
    def _():
        rec[0] = own_chip[...]
        rec[1] = next_chip[...]


def iota(axis, shape=(ROWS, 128)):
    return lax.broadcasted_iota(jnp.int32, shape, axis)


def next_lane(tile):
    return jnp.where(iota(1) < 127, pltpu.roll(tile, 127, 1), 0.0)


def previous_lane(tile):
    return jnp.where(iota(1) > 0, pltpu.roll(tile, 1, 1), 0.0)


def node_pairs(tile, last=True):
    lower = pltpu.roll(tile, 1, 0)
    parts = {}
    for name, part in (("s", tile + lower), ("d", tile - lower)):
        upper = next_lane(part)
        parts[name + "s"] = part + upper
        if last or name == "s":
            parts[name + "d"] = upper - part
    return parts


def element_modes(lower, upper):
    modes = []
    for below, above in zip(lower, upper):
        mode = {"d" + pair: above[pair] - below[pair] for pair in above}
        mode.update({"s" + pair: above[pair] + below[pair] for pair in above if pair != "ss"})
        modes.append(mode)
    return modes


def element_loads(modes, moduli):
    lame, both, lame_third, shear_third, cubic = moduli
    u, v, w = modes
    fu, fv, fw = {}, {}, {}
    trace = lame * (u["dss"] + v["sds"] + w["ssd"])
    twice = both + both
    fu["dss"] = trace + twice * u["dss"]
    fv["sds"] = trace + twice * v["sds"]
    fw["ssd"] = trace + twice * w["ssd"]
    fw["sds"] = fv["ssd"] = both * (w["sds"] + v["ssd"])
    fw["dss"] = fu["ssd"] = both * (w["dss"] + u["ssd"])
    fv["dss"] = fu["sds"] = both * (v["dss"] + u["sds"])
    triple = 3.0 * shear_third
    part = lame_third * (u["dds"] + w["sdd"])
    fu["dds"] = part + triple * u["dds"]
    fw["sdd"] = part + triple * w["sdd"]
    part = lame_third * (v["dds"] + w["dsd"])
    fv["dds"] = part + triple * v["dds"]
    fw["dsd"] = part + triple * w["dsd"]
    part = lame_third * (u["dsd"] + v["sdd"])
    fu["dsd"] = part + triple * u["dsd"]
    fv["sdd"] = part + triple * v["sdd"]
    part = w["dds"] + v["dsd"] + u["sdd"]
    fw["dds"] = shear_third * (part + w["dds"])
    fv["dsd"] = shear_third * (part + v["dsd"])
    fu["sdd"] = shear_third * (part + u["sdd"])
    for mode, force in zip(modes, (fu, fv, fw)):
        force["ddd"] = cubic * mode["ddd"]
    return fu, fv, fw


def plus(a, b):
    return b if a is None else a if b is None else a + b


def to_nodes(forces):
    uppers, lowers = [], []
    for force in forces:
        upper, lower = {}, {}
        for pair in PAIRS:
            s, d = force.get("s" + pair), force.get("d" + pair)
            upper[pair] = plus(s, d)
            lower[pair] = None if s is None and d is None else (-d if s is None else s if d is None else s - d)
        uppers.append(upper)
        lowers.append(lower)
    return uppers, lowers


def node_force(pairs):
    along = {}
    for name in "sd":
        s, d = pairs[name + "s"], pairs[name + "d"]
        if d is None:
            along[name] = s + previous_lane(s)
        else:
            along[name] = (s - d) + previous_lane(s + d)
    return (along["s"] + along["d"]) + pltpu.roll(along["s"] - along["d"], ROWS - 1, 0)


def merged(first, second):
    return [{pair: plus(a[pair], b[pair]) for pair in PAIRS} for a, b in zip(first, second)]


def krylov_body(sides, rec, wide, table, basis, sums, vec, mask, moduli):
    blocks = (sides.at[0], rec.at[0], wide, rec.at[1], sides.at[1])
    for layer in range(LAYERS):
        block, place = blocks[layer // 2], layer % 2
        index = block[9 + place].astype(jnp.int32) + CLASSES
        lame, shear, arm = (pick(table, row, index) for row in range(3))
        moduli[0, layer] = lame
        moduli[1, layer] = shear + arm
        moduli[2, layer] = lame * (1.0 / 3.0)
        moduli[3, layer] = shear * (1.0 / 3.0)
        moduli[4, layer] = (lame + 4.0 * shear) * (1.0 / 9.0)
        mask[layer] = block[11 + place]
        if layer < LAYERS - 1:
            for comp in range(3):
                force = block[3 * comp + 1 + place]
                if place == 1:
                    force = force + blocks[layer // 2 + 1][3 * comp]
                vec[0, comp, layer] = mask[layer] * force

    def masked_pairs(step, layer):
        return [node_pairs(mask[layer] * vec[step, comp, layer]) for comp in range(3)]

    for step in range(ITERS - 1):
        below = masked_pairs(step, step)
        pending = None
        for layer in range(step + 1, LAYERS - 1 - step):
            above = masked_pairs(step, layer)
            loads = element_loads(element_modes(below, above), [moduli[k, layer] for k in range(5)])
            upper, lower = to_nodes(loads)
            if pending is not None:
                node = layer - 1
                free = mask[node]
                for comp, pairs in enumerate(merged(pending, lower)):
                    value = vec[step, comp, node]
                    image = free * node_force(pairs) + (1.0 - free) * value
                    vec[step + 1, comp, node] = SCALE * image
            pending = upper
            below = above

    last = ITERS - 1
    energy = jnp.zeros((8, 128), F32)
    below = masked_pairs(last, 3)
    for layer in (4, 5):
        above = masked_pairs(last, layer)
        modes = element_modes(below, above)
        loads = element_loads(modes, [moduli[k, layer] for k in range(5)])
        total = None
        for mode, force in zip(modes, loads):
            for name in force:
                total = plus(total, (mode[name] * force[name])[0:8])
        energy = energy + total
        for comp in range(3):
            value = vec[last, comp, layer, 0:8]
            energy = energy + (1.0 - mask[layer, 0:8]) * value * value
        below = above

    moments = []
    for k in range(MOMENTS - 1):
        total = None
        for comp in range(3):
            for layer in (4, 5):
                total = plus(total, vec[k // 2, comp, layer, 0:8] * vec[(k + 1) // 2, comp, layer, 0:8])
        moments.append(total)
    moments.append(SCALE * energy)
    row, lane = iota(0, (8, 128)), iota(1, (8, 128))
    rows = jnp.zeros((8, 128), F32)
    for k, total in enumerate(moments):
        rows = jnp.where(row == k, jnp.sum(total, axis=0, keepdims=True), rows)
    for step in (64, 32, 16):
        rows = rows + pltpu.roll(rows, step, 1)
    line = jnp.sum(jnp.where(lane // 16 == row, rows, 0.0), axis=0, keepdims=True)
    sums[...] = jnp.broadcast_to(line, sums.shape)
    for step in range(ITERS):
        for comp in range(3):
            for layer in range(3):
                basis[step, comp, layer] = vec[step, comp, 3 + layer]


def two_sum(a, b):
    total = a + b
    part = total - a
    return total, (a - (total - part)) + (b - part)


def settle(high, low):
    total = high + low
    return total, low - (total - high)


def add(a, b):
    total, rest = two_sum(a[0], b[0])
    return settle(total, rest + (a[1] + b[1]))


def halves(a):
    wide = 4097.0 * a
    high = wide - (wide - a)
    return high, a - high


def two_product(a, b):
    total = a * b
    (ah, al), (bh, bl) = halves(a), halves(b)
    return total, ((ah * bh - total) + ah * bl + al * bh) + al * bl


def multiply(a, b):
    total, rest = two_product(a[0], b[0])
    return settle(total, rest + (a[0] * b[1] + a[1] * b[0]))


def subtract(a, b):
    return add(a, (-b[0], -b[1]))


def invert(a):
    first = 1.0 / a[0]
    total, rest = two_product(a[0], first)
    return settle(first, first * (((1.0 - total) - rest) - a[1] * first))


def rolled(a, steps, axis):
    return tuple(pltpu.roll(part, steps, axis) for part in a)


def over_rows(pair):
    for step in (4, 2, 1):
        pair = add(pair, rolled(pair, step, 0))
    return pair


def total_of(pairs):
    while len(pairs) > 1:
        pairs = [add(*pairs[k : k + 2]) if k + 1 < len(pairs) else pairs[k] for k in range(0, len(pairs), 2)]
    return pairs[0]


def middle_body(sums, out):
    pair = over_rows(total_of([(sums[k : k + 8], jnp.zeros((8, 128), F32)) for k in range(0, sums.shape[0], 8)]))
    high, low = add(pair, rolled(pair, 120, 1))
    line = jnp.where(iota(1, (8, 128)) % 16 < 8, high, pltpu.roll(low, 8, 1))
    for k in range(0, out.shape[0], 8):
        count = min(8, out.shape[0] - k)
        out[k : k + count] = line[0:count]


def final_body(sums, basis, own, table, displacement, viscous_next):
    pairs = []
    for k in range(sums.shape[0] // 8):
        tile = sums[8 * k : 8 * k + 8]
        pairs.append((tile, pltpu.roll(tile, 120, 1)))
    pair = over_rows(total_of(pairs))
    for step in (4, 2, 1):
        pair = add(pair, rolled(pair, 128 - step, 1))

    def moment(k):
        index = jnp.full((8, 128), 16 * k, jnp.int32)
        return tuple(jnp.take_along_axis(part, index, axis=1, mode="promise_in_bounds") for part in pair)

    moments = [moment(k) for k in range(MOMENTS)]
    matrix = [[moments[i + j + 1] for j in range(i + 1)] for i in range(ITERS)]
    value = moments[:ITERS]
    ratio = {}
    inverse = []
    for k in range(ITERS):
        pivot = matrix[k][k]
        kept = pivot[0] > TINY_PIVOT * moments[2 * k + 1][0]
        inverse.append(tuple(jnp.where(kept, part, 0.0) for part in invert(pivot)))
        for i in range(k + 1, ITERS):
            ratio[i, k] = multiply(matrix[i][k], inverse[k])
            for j in range(k + 1, i + 1):
                matrix[i][j] = subtract(matrix[i][j], multiply(ratio[i, k], matrix[j][k]))
            value[i] = subtract(value[i], multiply(ratio[i, k], value[k]))
    value = [multiply(value[k], inverse[k]) for k in range(ITERS)]
    for k in reversed(range(ITERS)):
        for i in range(k):
            value[i] = subtract(value[i], multiply(ratio[k, i], value[k]))
    weights = [SCALE * jnp.concatenate([v[0], v[0]], axis=0) for v in value]

    pairs = []
    for layer in range(3):
        fields = []
        for comp in range(3):
            total = weights[0] * basis[0, comp, layer]
            for step in range(1, ITERS):
                total = total + weights[step] * basis[step, comp, layer]
            if layer > 0:
                displacement[comp, layer - 1] = total[0:8]
            fields.append(node_pairs(total, last=False))
        pairs.append(fields)
    for layer in range(2):
        u, v, w = element_modes(pairs[layer], pairs[layer + 1])
        strain = (
            0.25 * u["dss"],
            0.25 * v["sds"],
            0.25 * w["ssd"],
            0.125 * (w["sds"] + v["ssd"]),
            0.125 * (w["dss"] + u["ssd"]),
            0.125 * (v["dss"] + u["sds"]),
        )
        index = own[18 + layer].astype(jnp.int32) + CLASSES
        entries = jnp.broadcast_to(table[3:4], (8, 128))
        retain = jnp.take_along_axis(entries, index, axis=1, mode="promise_in_bounds")
        for part in range(6):
            old = own[6 + 2 * part + layer]
            viscous_next[part, layer] = retain * old + (1.0 - retain) * strain[part][0:8]


def shifted(value, axes, count, steps):
    pairs = [(i, i + steps) for i in range(count) if 0 <= i + steps < count]
    return lax.ppermute(value, axes, pairs)


def swapped(value, axes, count, start):
    lower = [i for i in range(start, count - 1, 2)]
    return lax.ppermute(value, axes, [(i, i + 1) for i in lower] + [(i + 1, i) for i in lower])


def solution(mesh):
    count_x, count_z = mesh.shape["gx"], mesh.shape["gy"]
    along = min(8, count_x // 2)
    across = count_x // (2 * along)
    grid = Mesh(mesh.devices.reshape(across, along, 2, count_z), ("y", "x", "core", "z"))
    chips = along * across

    def shards(load, viscous, material, free_nodes, moduli_table, relax_time):
        def parity(axes):
            return (lax.axis_index(axes) % 2).astype(jnp.int32).reshape(1)

        odd_chip, core = parity("x"), parity("core")
        own, low, high, table = call(
            pack_body,
            (SDS((22, 8, 128), F32), SDS((11, 8, 128), F32), SDS((11, 8, 128), F32), SDS((8, 128), F32)),
            6,
            scratch=(
                pltpu.VMEM((2, 8, 128), jnp.int32),
                pltpu.VMEM((2, 8, 128), jnp.int32),
                pltpu.VMEM((3, CLASSES), F32),
                pltpu.VMEM((1, CLASSES), F32),
                pltpu.SemaphoreType.DMA((6,)),
            ),
            spec=HBM,
        )(
            *(
                pltpu.with_memory_space_constraint(value, pltpu.HBM)
                for value in (
                    load.reshape(6, 8, 128),
                    viscous.reshape(12, 8, 128),
                    material,
                    free_nodes,
                    moduli_table,
                    relax_time.reshape(1, CLASSES),
                )
            )
        )
        below = shifted(high, ("z",), count_z, 1)
        above = shifted(low, ("z",), count_z, -1)
        wide = call(widen_body, SDS((BLOCK, ROWS, 128), F32), 4)(own, above, below, table)
        first = swapped(wide, ("y", "x"), chips, 0)
        second = swapped(wide, ("y", "x"), chips, 1)
        own_chip = swapped(wide, ("y", "x", "core"), count_x, 0)
        next_chip = swapped(wide, ("y", "x", "core"), count_x, 1)
        sides, taken = call(
            order_body,
            (SDS((2, BLOCK, ROWS, 128), F32), SDS((2, BLOCK, ROWS, 128), F32)),
            6,
            scalars=2,
        )(core, odd_chip, first, second, own_chip, next_chip)
        near, far = along * count_z, 2 * across
        basis, sums = call(
            krylov_body,
            (SDS((ITERS, 3, 3, ROWS, 128), F32), SDS((near, 128), F32)),
            4,
            scratch=(
                pltpu.VMEM((ITERS, 3, LAYERS, ROWS, 128), F32),
                pltpu.VMEM((LAYERS, ROWS, 128), F32),
                pltpu.VMEM((5, LAYERS, ROWS, 128), F32),
            ),
            flops=20000000,
        )(sides, taken, wide, table)
        group = lax.all_to_all(sums.reshape(near, 1, 128), ("x", "z"), 0, 0)
        partial = call(middle_body, SDS((far, 128), F32), 1)(group.reshape(near, 128))
        everything = lax.all_to_all(partial.reshape(far, 1, 128), ("y", "core"), 0, 0)
        return tuple(
            call(final_body, (SDS((3, 2, 8, 128), F32), SDS((6, 2, 8, 128), F32)), 4)(
                jnp.pad(everything.reshape(far, 128), ((0, -far % 8), (0, 0))), basis, own, table
            )
        )

    return jax.shard_map(
        shards,
        mesh=grid,
        in_specs=(
            P(None, ("y", "x", "core"), "z", None),
            P(None, ("y", "x", "core"), "z", None),
            P(("y", "x", "core"), "z", None),
            P(("y", "x", "core"), "z", None),
            P(),
            P(),
        ),
        out_specs=(P(None, ("y", "x", "core"), "z", None), P(None, ("y", "x", "core"), "z", None)),
        check_vma=False,
    )
```

```python
import math

import jax
import jax.numpy as jnp
from jax import lax
from jax.experimental import pallas as pl
from jax.experimental.pallas import tpu as pltpu
from jax.sharding import Mesh, PartitionSpec as P

ITERS = 4
ROWS = 16
LAYERS = 10
BLOCK = 13
HALF = 7
CLASSES = 16
MOMENTS = 2 * ITERS
SCALE = 1.0 / 32.0
TINY_PIVOT = 1e-9

F32 = jnp.float32
SDS = jax.ShapeDtypeStruct
VMEM = pl.BlockSpec(memory_space=pltpu.VMEM)
SMEM = pl.BlockSpec(memory_space=pltpu.SMEM)
HBM = pl.BlockSpec(memory_space=pltpu.HBM)
PAIRS = ("ss", "sd", "ds", "dd")


def call(body, out_shape, n_in, scratch=(), spec=VMEM, scalars=0, flops=100000):
    many = isinstance(out_shape, (list, tuple))
    return pl.pallas_call(
        body,
        out_shape=out_shape,
        in_specs=[SMEM] * scalars + [spec] * (n_in - scalars),
        out_specs=[VMEM] * len(out_shape) if many else VMEM,
        scratch_shapes=list(scratch),
        compiler_params=pltpu.CompilerParams(vmem_limit_bytes=24 * 1024 * 1024),
        cost_estimate=pl.CostEstimate(flops=flops, bytes_accessed=100000, transcendentals=0),
    )


def pick(table, row, index):
    entries = jnp.broadcast_to(table[row : row + 1], index.shape)
    return jnp.take_along_axis(entries, index, axis=1, mode="promise_in_bounds")


def pack_body(
    load, viscous, material, free, moduli, relax, own, part, low, high, table, loads, kinds, frees, entries, times, done
):
    pairs = (
        (load, loads),
        (viscous, own.at[0:12]),
        (material, kinds),
        (free, frees),
        (moduli, entries),
        (relax, times),
    )
    copies = [pltpu.make_async_copy(source, target, done.at[k]) for k, (source, target) in enumerate(pairs)]
    for copy in copies:
        copy.start()
    for copy in copies:
        copy.wait()
    time = times[...]
    retain = time / (time + 1.0)
    table[...] = jnp.zeros((8, 128), F32)
    table[0:1, 0:CLASSES] = entries[0:1] * (1.0 / 16.0)
    table[1:2, 0:CLASSES] = entries[1:2] * (1.0 / 16.0)
    table[2:3, 0:CLASSES] = (entries[2:3] * retain) * (1.0 / 16.0)
    table[3:4, 0:CLASSES] = retain
    nothing = jnp.zeros((8, 128), F32)

    def tall(tile):
        return jnp.concatenate([tile, nothing], axis=0)

    pending = None
    for layer in range(2):
        kind = kinds[layer]
        own[12 + layer] = kind.astype(F32) - float(CLASSES)
        part[9 + layer] = tall(own[12 + layer])
        part[11 + layer] = tall(frees[layer].astype(F32))
        factor = 8.0 * pick(table, 2, kind)
        xx, yy, zz, yz, xz, xy = (tall(factor * own[2 * number + layer]) for number in range(6))
        forces = (
            {"dss": xx, "ssd": xz, "sds": xy},
            {"sds": yy, "ssd": yz, "dss": xy},
            {"ssd": zz, "sds": yz, "dss": xz},
        )
        upper, lower = to_nodes(forces)
        pairs = lower if pending is None else merged(pending, lower)
        for comp in range(3):
            force = node_force(pairs[comp])
            part[3 * comp + layer] = force if layer == 0 else tall(loads[2 * comp]) + force
        pending = upper
    for comp in range(3):
        part[3 * comp + 2] = tall(loads[2 * comp + 1]) + node_force(pending[comp])
    row = lax.broadcasted_iota(jnp.int32, (8, 128), 0)
    for pair in range(HALF):
        firsts, lasts = [], []
        for k in (2 * pair, 2 * pair + 1):
            if k >= BLOCK:
                firsts.append(nothing)
                lasts.append(nothing)
                continue
            tile = part[k]
            firsts.append(pltpu.roll(tile, 1, 0)[0:8] if k < 9 else tile[0:8])
            lasts.append(tile[0:8])
        low[pair] = jnp.where(row < 4, firsts[0], pltpu.roll(firsts[1], 4, 0))
        high[pair] = jnp.where(row < 4, pltpu.roll(lasts[0], 4, 0), lasts[1])


def widen_body(part, above, below, wide):
    row = lax.broadcasted_iota(jnp.int32, (8, 128), 0)
    nothing = jnp.zeros((8, 128), F32)
    for k in range(BLOCK):
        upper, lower = above[k // 2], below[k // 2]
        if k % 2 == 0:
            lower = pltpu.roll(lower, 4, 0)
        else:
            upper = pltpu.roll(upper, 4, 0)
        if k < 9:
            first = jnp.concatenate([jnp.where(row < 4, upper, 0.0), nothing], axis=0)
            last = jnp.concatenate([nothing, jnp.where(row < 4, 0.0, lower)], axis=0)
            wide[k] = part[k] + (pltpu.roll(first, 7, 0) + last)
        else:
            wide[k, 0:8] = part[k, 0:8]
            wide[k, 8:16] = jnp.where(row < 4, upper, lower)


def choose_body(core, odd, wide, first, second, given, sides):
    @pl.when(odd[0] == 0)
    def _():
        sides[0] = second[...]
        sides[1] = first[...]

    @pl.when(odd[0] != 0)
    def _():
        sides[0] = first[...]
        sides[1] = second[...]

    @pl.when(core[0] == 0)
    def _():
        given[0] = wide[...]
        given[1] = sides[1]

    @pl.when(core[0] != 0)
    def _():
        given[0] = sides[0]
        given[1] = wide[...]


def iota(axis, shape=(ROWS, 128)):
    return lax.broadcasted_iota(jnp.int32, shape, axis)


def next_lane(tile):
    return jnp.where(iota(1) < 127, pltpu.roll(tile, 127, 1), 0.0)


def previous_lane(tile):
    return jnp.where(iota(1) > 0, pltpu.roll(tile, 1, 1), 0.0)


def node_pairs(tile, last=True):
    lower = pltpu.roll(tile, 1, 0)
    parts = {}
    for name, part in (("s", tile + lower), ("d", tile - lower)):
        upper = next_lane(part)
        parts[name + "s"] = part + upper
        if last or name == "s":
            parts[name + "d"] = upper - part
    return parts


def element_modes(lower, upper):
    modes = []
    for below, above in zip(lower, upper):
        mode = {"d" + pair: above[pair] - below[pair] for pair in above}
        mode.update({"s" + pair: above[pair] + below[pair] for pair in above if pair != "ss"})
        modes.append(mode)
    return modes


def element_loads(modes, moduli):
    lame, both, lame_third, shear_third, cubic = moduli
    u, v, w = modes
    fu, fv, fw = {}, {}, {}
    trace = lame * (u["dss"] + v["sds"] + w["ssd"])
    twice = both + both
    fu["dss"] = trace + twice * u["dss"]
    fv["sds"] = trace + twice * v["sds"]
    fw["ssd"] = trace + twice * w["ssd"]
    fw["sds"] = fv["ssd"] = both * (w["sds"] + v["ssd"])
    fw["dss"] = fu["ssd"] = both * (w["dss"] + u["ssd"])
    fv["dss"] = fu["sds"] = both * (v["dss"] + u["sds"])
    triple = 3.0 * shear_third
    part = lame_third * (u["dds"] + w["sdd"])
    fu["dds"] = part + triple * u["dds"]
    fw["sdd"] = part + triple * w["sdd"]
    part = lame_third * (v["dds"] + w["dsd"])
    fv["dds"] = part + triple * v["dds"]
    fw["dsd"] = part + triple * w["dsd"]
    part = lame_third * (u["dsd"] + v["sdd"])
    fu["dsd"] = part + triple * u["dsd"]
    fv["sdd"] = part + triple * v["sdd"]
    part = w["dds"] + v["dsd"] + u["sdd"]
    fw["dds"] = shear_third * (part + w["dds"])
    fv["dsd"] = shear_third * (part + v["dsd"])
    fu["sdd"] = shear_third * (part + u["sdd"])
    for mode, force in zip(modes, (fu, fv, fw)):
        force["ddd"] = cubic * mode["ddd"]
    return fu, fv, fw


def plus(a, b):
    return b if a is None else a if b is None else a + b


def to_nodes(forces):
    uppers, lowers = [], []
    for force in forces:
        upper, lower = {}, {}
        for pair in PAIRS:
            s, d = force.get("s" + pair), force.get("d" + pair)
            upper[pair] = plus(s, d)
            lower[pair] = None if s is None and d is None else (-d if s is None else s if d is None else s - d)
        uppers.append(upper)
        lowers.append(lower)
    return uppers, lowers


def node_force(pairs):
    along = {}
    for name in "sd":
        s, d = pairs[name + "s"], pairs[name + "d"]
        if d is None:
            along[name] = s + previous_lane(s)
        else:
            along[name] = (s - d) + previous_lane(s + d)
    return (along["s"] + along["d"]) + pltpu.roll(along["s"] - along["d"], ROWS - 1, 0)


def merged(first, second):
    return [{pair: plus(a[pair], b[pair]) for pair in PAIRS} for a, b in zip(first, second)]


def krylov_body(sides, rec, wide, table, basis, sums, vec, mask, moduli):
    blocks = (sides.at[0], rec.at[0], wide, rec.at[1], sides.at[1])
    for layer in range(LAYERS):
        block, place = blocks[layer // 2], layer % 2
        index = block[9 + place].astype(jnp.int32) + CLASSES
        lame, shear, arm = (pick(table, row, index) for row in range(3))
        moduli[0, layer] = lame
        moduli[1, layer] = shear + arm
        moduli[2, layer] = lame * (1.0 / 3.0)
        moduli[3, layer] = shear * (1.0 / 3.0)
        moduli[4, layer] = (lame + 4.0 * shear) * (1.0 / 9.0)
        mask[layer] = block[11 + place]
        if layer < LAYERS - 1:
            for comp in range(3):
                force = block[3 * comp + 1 + place]
                if place == 1:
                    force = force + blocks[layer // 2 + 1][3 * comp]
                vec[0, comp, layer] = mask[layer] * force

    def masked_pairs(step, layer):
        return [node_pairs(mask[layer] * vec[step, comp, layer]) for comp in range(3)]

    for step in range(ITERS - 1):
        below = masked_pairs(step, step)
        pending = None
        for layer in range(step + 1, LAYERS - 1 - step):
            above = masked_pairs(step, layer)
            loads = element_loads(element_modes(below, above), [moduli[k, layer] for k in range(5)])
            upper, lower = to_nodes(loads)
            if pending is not None:
                node = layer - 1
                free = mask[node]
                for comp, pairs in enumerate(merged(pending, lower)):
                    value = vec[step, comp, node]
                    image = free * node_force(pairs) + (1.0 - free) * value
                    vec[step + 1, comp, node] = SCALE * image
            pending = upper
            below = above

    last = ITERS - 1
    energy = jnp.zeros((8, 128), F32)
    below = masked_pairs(last, 3)
    for layer in (4, 5):
        above = masked_pairs(last, layer)
        modes = element_modes(below, above)
        loads = element_loads(modes, [moduli[k, layer] for k in range(5)])
        total = None
        for mode, force in zip(modes, loads):
            for name in force:
                total = plus(total, (mode[name] * force[name])[0:8])
        energy = energy + total
        for comp in range(3):
            value = vec[last, comp, layer, 0:8]
            energy = energy + (1.0 - mask[layer, 0:8]) * value * value
        below = above

    moments = []
    for k in range(MOMENTS - 1):
        total = None
        for comp in range(3):
            for layer in (4, 5):
                total = plus(total, vec[k // 2, comp, layer, 0:8] * vec[(k + 1) // 2, comp, layer, 0:8])
        moments.append(total)
    moments.append(SCALE * energy)
    row, lane = iota(0, (8, 128)), iota(1, (8, 128))
    rows = jnp.zeros((8, 128), F32)
    for k, total in enumerate(moments):
        rows = jnp.where(row == k, jnp.sum(total, axis=0, keepdims=True), rows)
    for step in (64, 32, 16):
        rows = rows + pltpu.roll(rows, step, 1)
    line = jnp.sum(jnp.where(lane // 16 == row, rows, 0.0), axis=0, keepdims=True)
    sums[...] = jnp.broadcast_to(line, sums.shape)
    for step in range(ITERS):
        for comp in range(3):
            for layer in range(3):
                basis[step, comp, layer] = vec[step, comp, 3 + layer]


def two_sum(a, b):
    total = a + b
    part = total - a
    return total, (a - (total - part)) + (b - part)


def settle(high, low):
    total = high + low
    return total, low - (total - high)


def add(a, b):
    total, rest = two_sum(a[0], b[0])
    return settle(total, rest + (a[1] + b[1]))


def halves(a):
    wide = 4097.0 * a
    high = wide - (wide - a)
    return high, a - high


def two_product(a, b):
    total = a * b
    (ah, al), (bh, bl) = halves(a), halves(b)
    return total, ((ah * bh - total) + ah * bl + al * bh) + al * bl


def multiply(a, b):
    total, rest = two_product(a[0], b[0])
    return settle(total, rest + (a[0] * b[1] + a[1] * b[0]))


def subtract(a, b):
    return add(a, (-b[0], -b[1]))


def invert(a):
    first = 1.0 / a[0]
    total, rest = two_product(a[0], first)
    return settle(first, first * (((1.0 - total) - rest) - a[1] * first))


def rolled(a, steps, axis):
    return tuple(pltpu.roll(part, steps, axis) for part in a)


def over_rows(pair):
    for step in (4, 2, 1):
        pair = add(pair, rolled(pair, step, 0))
    return pair


def total_of(pairs):
    while len(pairs) > 1:
        pairs = [add(*pairs[k : k + 2]) if k + 1 < len(pairs) else pairs[k] for k in range(0, len(pairs), 2)]
    return pairs[0]


def middle_body(sums, out):
    pair = over_rows(total_of([(sums[k : k + 8], jnp.zeros((8, 128), F32)) for k in range(0, sums.shape[0], 8)]))
    high, low = add(pair, rolled(pair, 120, 1))
    line = jnp.where(iota(1, (8, 128)) % 16 < 8, high, pltpu.roll(low, 8, 1))
    for k in range(0, out.shape[0], 8):
        count = min(8, out.shape[0] - k)
        out[k : k + count] = line[0:count]


def final_body(sums, basis, own, table, displacement, viscous_next):
    pairs = []
    for k in range(sums.shape[0] // 8):
        tile = sums[8 * k : 8 * k + 8]
        pairs.append((tile, pltpu.roll(tile, 120, 1)))
    pair = over_rows(total_of(pairs))
    for step in (4, 2, 1):
        pair = add(pair, rolled(pair, 128 - step, 1))

    def moment(k):
        index = jnp.full((8, 128), 16 * k, jnp.int32)
        return tuple(jnp.take_along_axis(part, index, axis=1, mode="promise_in_bounds") for part in pair)

    moments = [moment(k) for k in range(MOMENTS)]
    matrix = [[moments[i + j + 1] for j in range(i + 1)] for i in range(ITERS)]
    value = moments[:ITERS]
    ratio = {}
    inverse = []
    for k in range(ITERS):
        pivot = matrix[k][k]
        kept = pivot[0] > TINY_PIVOT * moments[2 * k + 1][0]
        inverse.append(tuple(jnp.where(kept, part, 0.0) for part in invert(pivot)))
        for i in range(k + 1, ITERS):
            ratio[i, k] = multiply(matrix[i][k], inverse[k])
            for j in range(k + 1, i + 1):
                matrix[i][j] = subtract(matrix[i][j], multiply(ratio[i, k], matrix[j][k]))
            value[i] = subtract(value[i], multiply(ratio[i, k], value[k]))
    value = [multiply(value[k], inverse[k]) for k in range(ITERS)]
    for k in reversed(range(ITERS)):
        for i in range(k):
            value[i] = subtract(value[i], multiply(ratio[k, i], value[k]))
    weights = [SCALE * jnp.concatenate([v[0], v[0]], axis=0) for v in value]

    pairs = []
    for layer in range(3):
        fields = []
        for comp in range(3):
            total = weights[0] * basis[0, comp, layer]
            for step in range(1, ITERS):
                total = total + weights[step] * basis[step, comp, layer]
            if layer > 0:
                displacement[comp, layer - 1] = total[0:8]
            fields.append(node_pairs(total, last=False))
        pairs.append(fields)
    for layer in range(2):
        u, v, w = element_modes(pairs[layer], pairs[layer + 1])
        strain = (
            0.25 * u["dss"],
            0.25 * v["sds"],
            0.25 * w["ssd"],
            0.125 * (w["sds"] + v["ssd"]),
            0.125 * (w["dss"] + u["ssd"]),
            0.125 * (v["dss"] + u["sds"]),
        )
        index = own[12 + layer].astype(jnp.int32) + CLASSES
        entries = jnp.broadcast_to(table[3:4], (8, 128))
        retain = jnp.take_along_axis(entries, index, axis=1, mode="promise_in_bounds")
        for part in range(6):
            old = own[2 * part + layer]
            viscous_next[part, layer] = retain * old + (1.0 - retain) * strain[part][0:8]


def shifted(value, axes, count, steps):
    pairs = [(i, i + steps) for i in range(count) if 0 <= i + steps < count]
    return lax.ppermute(value, axes, pairs)


def swapped(value, axes, count, start):
    lower = [i for i in range(start, count - 1, 2)]
    return lax.ppermute(value, axes, [(i, i + 1) for i in lower] + [(i + 1, i) for i in lower])


def solution(mesh):
    count_x, count_z = mesh.shape["gx"], mesh.shape["gy"]
    along = min(8, count_x // 2)
    across = count_x // (2 * along)
    grid = Mesh(mesh.devices.reshape(across, along, 2, count_z), ("y", "x", "core", "z"))
    chips = along * across

    def shards(load, viscous, material, free_nodes, moduli_table, relax_time):
        def parity(axes):
            return (lax.axis_index(axes) % 2).astype(jnp.int32).reshape(1)

        odd_chip, core = parity("x"), parity("core")
        own, part, low, high, table = call(
            pack_body,
            (
                SDS((14, 8, 128), F32),
                SDS((BLOCK, ROWS, 128), F32),
                SDS((HALF, 8, 128), F32),
                SDS((HALF, 8, 128), F32),
                SDS((8, 128), F32),
            ),
            6,
            scratch=(
                pltpu.VMEM((6, 8, 128), F32),
                pltpu.VMEM((2, 8, 128), jnp.int32),
                pltpu.VMEM((2, 8, 128), jnp.int32),
                pltpu.VMEM((3, CLASSES), F32),
                pltpu.VMEM((1, CLASSES), F32),
                pltpu.SemaphoreType.DMA((6,)),
            ),
            spec=HBM,
        )(
            *(
                pltpu.with_memory_space_constraint(value, pltpu.HBM)
                for value in (
                    load.reshape(6, 8, 128),
                    viscous.reshape(12, 8, 128),
                    material,
                    free_nodes,
                    moduli_table,
                    relax_time.reshape(1, CLASSES),
                )
            )
        )
        below = shifted(high, ("z",), count_z, 1)
        above = shifted(low, ("z",), count_z, -1)
        wide = call(widen_body, SDS((BLOCK, ROWS, 128), F32), 3)(part, above, below)
        first = swapped(wide, ("y", "x"), chips, 0)
        second = swapped(wide, ("y", "x"), chips, 1)
        given, sides = call(
            choose_body,
            (SDS((2, BLOCK, ROWS, 128), F32), SDS((2, BLOCK, ROWS, 128), F32)),
            5,
            scalars=2,
        )(core, odd_chip, wide, first, second)
        taken = lax.ppermute(given, ("core",), [(0, 1), (1, 0)])
        near, far = along * count_z, 2 * across
        basis, sums = call(
            krylov_body,
            (SDS((ITERS, 3, 3, ROWS, 128), F32), SDS((near, 128), F32)),
            4,
            scratch=(
                pltpu.VMEM((ITERS, 3, LAYERS, ROWS, 128), F32),
                pltpu.VMEM((LAYERS, ROWS, 128), F32),
                pltpu.VMEM((5, LAYERS, ROWS, 128), F32),
            ),
            flops=20000000,
        )(sides, taken, wide, table)
        group = lax.all_to_all(sums.reshape(near, 1, 128), ("x", "z"), 0, 0)
        partial = call(middle_body, SDS((far, 128), F32), 1)(group.reshape(near, 128))
        everything = lax.all_to_all(partial.reshape(far, 1, 128), ("y", "core"), 0, 0)
        return tuple(
            call(final_body, (SDS((3, 2, 8, 128), F32), SDS((6, 2, 8, 128), F32)), 4)(
                jnp.pad(everything.reshape(far, 128), ((0, -far % 8), (0, 0))), basis, own, table
            )
        )

    return jax.shard_map(
        shards,
        mesh=grid,
        in_specs=(
            P(None, ("y", "x", "core"), "z", None),
            P(None, ("y", "x", "core"), "z", None),
            P(("y", "x", "core"), "z", None),
            P(("y", "x", "core"), "z", None),
            P(),
            P(),
        ),
        out_specs=(P(None, ("y", "x", "core"), "z", None), P(None, ("y", "x", "core"), "z", None)),
        check_vma=False,
    )
```

```python
import math

import jax
import jax.numpy as jnp
from jax import lax
from jax.experimental import pallas as pl
from jax.experimental.pallas import tpu as pltpu
from jax.sharding import Mesh, PartitionSpec as P

ITERS = 4
ROWS = 16
LAYERS = 10
FIELDS = 11
BLOCK = 13
CLASSES = 16
MOMENTS = 2 * ITERS
SCALE = 1.0 / 32.0
TINY_PIVOT = 1e-9

F32 = jnp.float32
SDS = jax.ShapeDtypeStruct
VMEM = pl.BlockSpec(memory_space=pltpu.VMEM)
SMEM = pl.BlockSpec(memory_space=pltpu.SMEM)
HBM = pl.BlockSpec(memory_space=pltpu.HBM)
PAIRS = ("ss", "sd", "ds", "dd")


def call(body, out_shape, n_in, scratch=(), spec=VMEM, scalars=0, flops=100000):
    many = isinstance(out_shape, (list, tuple))
    return pl.pallas_call(
        body,
        out_shape=out_shape,
        in_specs=[SMEM] * scalars + [spec] * (n_in - scalars),
        out_specs=[VMEM] * len(out_shape) if many else VMEM,
        scratch_shapes=list(scratch),
        compiler_params=pltpu.CompilerParams(vmem_limit_bytes=24 * 1024 * 1024),
        cost_estimate=pl.CostEstimate(flops=flops, bytes_accessed=100000, transcendentals=0),
    )


def pack_body(load, viscous, material, free, moduli, relax, own, low, high, table, kinds, frees, entries, times, done):
    pairs = (
        (load, own.at[0:6]),
        (viscous, own.at[6:18]),
        (material, kinds),
        (free, frees),
        (moduli, entries),
        (relax, times),
    )
    copies = [pltpu.make_async_copy(source, target, done.at[k]) for k, (source, target) in enumerate(pairs)]
    for copy in copies:
        copy.start()
    for copy in copies:
        copy.wait()
    row = lax.broadcasted_iota(jnp.int32, (8, 128), 0)
    for field in range(FIELDS):
        if field == 9:
            layers = [kinds[layer].astype(F32) - float(CLASSES) for layer in range(2)]
        elif field == 10:
            layers = [frees[layer].astype(F32) for layer in range(2)]
        else:
            layers = [own[2 * field + layer] for layer in range(2)]
        if field >= 9:
            for layer in range(2):
                own[2 * field + layer] = layers[layer]
        low[field] = jnp.where(row < 4, layers[0], pltpu.roll(layers[1], 4, 0))
        high[field] = jnp.where(row < 4, pltpu.roll(layers[0], 4, 0), layers[1])
    time = times[...]
    retain = time / (time + 1.0)
    table[...] = jnp.zeros((8, 128), F32)
    table[0:1, 0:CLASSES] = entries[0:1] * (1.0 / 16.0)
    table[1:2, 0:CLASSES] = entries[1:2] * (1.0 / 16.0)
    table[2:3, 0:CLASSES] = (entries[2:3] * retain) * (1.0 / 16.0)
    table[3:4, 0:CLASSES] = retain


def pick(table, row, index):
    entries = jnp.broadcast_to(table[row : row + 1], index.shape)
    return jnp.take_along_axis(entries, index, axis=1, mode="promise_in_bounds")


def widen_body(own, above, below, table, wide):
    row = lax.broadcasted_iota(jnp.int32, (8, 128), 0)

    def rows(field):
        upper, lower = above[field], below[field]
        halos = (
            jnp.where(row < 4, upper, pltpu.roll(lower, 4, 0)),
            jnp.where(row < 4, pltpu.roll(upper, 4, 0), lower),
        )
        return [jnp.concatenate([own[2 * field + layer], halos[layer]], axis=0) for layer in range(2)]

    fields = [rows(field) for field in range(FIELDS)]
    for layer in range(2):
        wide[9 + layer] = fields[9][layer]
        wide[11 + layer] = fields[10][layer]
    pending = None
    for layer in range(2):
        index = fields[9][layer].astype(jnp.int32) + CLASSES
        factor = 8.0 * pick(table, 2, index)
        xx, yy, zz, yz, xz, xy = (factor * fields[3 + part][layer] for part in range(6))
        forces = (
            {"dss": xx, "ssd": xz, "sds": xy},
            {"sds": yy, "ssd": yz, "dss": xy},
            {"ssd": zz, "sds": yz, "dss": xz},
        )
        upper, lower = to_nodes(forces)
        pairs = lower if pending is None else merged(pending, lower)
        for comp in range(3):
            force = node_force(pairs[comp])
            wide[3 * comp + layer] = force if layer == 0 else fields[comp][0] + force
        pending = upper
    for comp in range(3):
        wide[3 * comp + 2] = fields[comp][1] + node_force(pending[comp])


def choose_body(core, odd, wide, first, second, given, sides):
    @pl.when(odd[0] == 0)
    def _():
        sides[0] = second[...]
        sides[1] = first[...]

    @pl.when(odd[0] != 0)
    def _():
        sides[0] = first[...]
        sides[1] = second[...]

    @pl.when(core[0] == 0)
    def _():
        given[0] = wide[...]
        given[1] = sides[1]

    @pl.when(core[0] != 0)
    def _():
        given[0] = sides[0]
        given[1] = wide[...]


def iota(axis, shape=(ROWS, 128)):
    return lax.broadcasted_iota(jnp.int32, shape, axis)


def next_lane(tile):
    return jnp.where(iota(1) < 127, pltpu.roll(tile, 127, 1), 0.0)


def previous_lane(tile):
    return jnp.where(iota(1) > 0, pltpu.roll(tile, 1, 1), 0.0)


def node_pairs(tile, last=True):
    lower = pltpu.roll(tile, 1, 0)
    parts = {}
    for name, part in (("s", tile + lower), ("d", tile - lower)):
        upper = next_lane(part)
        parts[name + "s"] = part + upper
        if last or name == "s":
            parts[name + "d"] = upper - part
    return parts


def element_modes(lower, upper):
    modes = []
    for below, above in zip(lower, upper):
        mode = {"d" + pair: above[pair] - below[pair] for pair in above}
        mode.update({"s" + pair: above[pair] + below[pair] for pair in above if pair != "ss"})
        modes.append(mode)
    return modes


def element_loads(modes, moduli):
    lame, both, lame_third, shear_third, cubic = moduli
    u, v, w = modes
    fu, fv, fw = {}, {}, {}
    trace = lame * (u["dss"] + v["sds"] + w["ssd"])
    twice = both + both
    fu["dss"] = trace + twice * u["dss"]
    fv["sds"] = trace + twice * v["sds"]
    fw["ssd"] = trace + twice * w["ssd"]
    fw["sds"] = fv["ssd"] = both * (w["sds"] + v["ssd"])
    fw["dss"] = fu["ssd"] = both * (w["dss"] + u["ssd"])
    fv["dss"] = fu["sds"] = both * (v["dss"] + u["sds"])
    triple = 3.0 * shear_third
    part = lame_third * (u["dds"] + w["sdd"])
    fu["dds"] = part + triple * u["dds"]
    fw["sdd"] = part + triple * w["sdd"]
    part = lame_third * (v["dds"] + w["dsd"])
    fv["dds"] = part + triple * v["dds"]
    fw["dsd"] = part + triple * w["dsd"]
    part = lame_third * (u["dsd"] + v["sdd"])
    fu["dsd"] = part + triple * u["dsd"]
    fv["sdd"] = part + triple * v["sdd"]
    part = w["dds"] + v["dsd"] + u["sdd"]
    fw["dds"] = shear_third * (part + w["dds"])
    fv["dsd"] = shear_third * (part + v["dsd"])
    fu["sdd"] = shear_third * (part + u["sdd"])
    for mode, force in zip(modes, (fu, fv, fw)):
        force["ddd"] = cubic * mode["ddd"]
    return fu, fv, fw


def plus(a, b):
    return b if a is None else a if b is None else a + b


def to_nodes(forces):
    uppers, lowers = [], []
    for force in forces:
        upper, lower = {}, {}
        for pair in PAIRS:
            s, d = force.get("s" + pair), force.get("d" + pair)
            upper[pair] = plus(s, d)
            lower[pair] = None if s is None and d is None else (-d if s is None else s if d is None else s - d)
        uppers.append(upper)
        lowers.append(lower)
    return uppers, lowers


def node_force(pairs):
    along = {}
    for name in "sd":
        s, d = pairs[name + "s"], pairs[name + "d"]
        if d is None:
            along[name] = s + previous_lane(s)
        else:
            along[name] = (s - d) + previous_lane(s + d)
    return (along["s"] + along["d"]) + pltpu.roll(along["s"] - along["d"], ROWS - 1, 0)


def merged(first, second):
    return [{pair: plus(a[pair], b[pair]) for pair in PAIRS} for a, b in zip(first, second)]


def krylov_body(sides, rec, wide, table, basis, sums, vec, mask, moduli):
    blocks = (sides.at[0], rec.at[0], wide, rec.at[1], sides.at[1])
    for layer in range(LAYERS):
        block, place = blocks[layer // 2], layer % 2
        index = block[9 + place].astype(jnp.int32) + CLASSES
        lame, shear, arm = (pick(table, row, index) for row in range(3))
        moduli[0, layer] = lame
        moduli[1, layer] = shear + arm
        moduli[2, layer] = lame * (1.0 / 3.0)
        moduli[3, layer] = shear * (1.0 / 3.0)
        moduli[4, layer] = (lame + 4.0 * shear) * (1.0 / 9.0)
        mask[layer] = block[11 + place]
        if layer < LAYERS - 1:
            for comp in range(3):
                force = block[3 * comp + 1 + place]
                if place == 1:
                    force = force + blocks[layer // 2 + 1][3 * comp]
                vec[0, comp, layer] = mask[layer] * force

    def masked_pairs(step, layer):
        return [node_pairs(mask[layer] * vec[step, comp, layer]) for comp in range(3)]

    for step in range(ITERS - 1):
        below = masked_pairs(step, step)
        pending = None
        for layer in range(step + 1, LAYERS - 1 - step):
            above = masked_pairs(step, layer)
            loads = element_loads(element_modes(below, above), [moduli[k, layer] for k in range(5)])
            upper, lower = to_nodes(loads)
            if pending is not None:
                node = layer - 1
                free = mask[node]
                for comp, pairs in enumerate(merged(pending, lower)):
                    value = vec[step, comp, node]
                    image = free * node_force(pairs) + (1.0 - free) * value
                    vec[step + 1, comp, node] = SCALE * image
            pending = upper
            below = above

    last = ITERS - 1
    energy = jnp.zeros((8, 128), F32)
    below = masked_pairs(last, 3)
    for layer in (4, 5):
        above = masked_pairs(last, layer)
        modes = element_modes(below, above)
        loads = element_loads(modes, [moduli[k, layer] for k in range(5)])
        total = None
        for mode, force in zip(modes, loads):
            for name in force:
                total = plus(total, (mode[name] * force[name])[0:8])
        energy = energy + total
        for comp in range(3):
            value = vec[last, comp, layer, 0:8]
            energy = energy + (1.0 - mask[layer, 0:8]) * value * value
        below = above

    moments = []
    for k in range(MOMENTS - 1):
        total = None
        for comp in range(3):
            for layer in (4, 5):
                total = plus(total, vec[k // 2, comp, layer, 0:8] * vec[(k + 1) // 2, comp, layer, 0:8])
        moments.append(total)
    moments.append(SCALE * energy)
    row, lane = iota(0, (8, 128)), iota(1, (8, 128))
    rows = jnp.zeros((8, 128), F32)
    for k, total in enumerate(moments):
        rows = jnp.where(row == k, jnp.sum(total, axis=0, keepdims=True), rows)
    for step in (64, 32, 16):
        rows = rows + pltpu.roll(rows, step, 1)
    line = jnp.sum(jnp.where(lane // 16 == row, rows, 0.0), axis=0, keepdims=True)
    sums[...] = jnp.broadcast_to(line, sums.shape)
    for step in range(ITERS):
        for comp in range(3):
            for layer in range(3):
                basis[step, comp, layer] = vec[step, comp, 3 + layer]


def two_sum(a, b):
    total = a + b
    part = total - a
    return total, (a - (total - part)) + (b - part)


def settle(high, low):
    total = high + low
    return total, low - (total - high)


def add(a, b):
    total, rest = two_sum(a[0], b[0])
    return settle(total, rest + (a[1] + b[1]))


def halves(a):
    wide = 4097.0 * a
    high = wide - (wide - a)
    return high, a - high


def two_product(a, b):
    total = a * b
    (ah, al), (bh, bl) = halves(a), halves(b)
    return total, ((ah * bh - total) + ah * bl + al * bh) + al * bl


def multiply(a, b):
    total, rest = two_product(a[0], b[0])
    return settle(total, rest + (a[0] * b[1] + a[1] * b[0]))


def subtract(a, b):
    return add(a, (-b[0], -b[1]))


def invert(a):
    first = 1.0 / a[0]
    total, rest = two_product(a[0], first)
    return settle(first, first * (((1.0 - total) - rest) - a[1] * first))


def rolled(a, steps, axis):
    return tuple(pltpu.roll(part, steps, axis) for part in a)


def over_rows(pair):
    for step in (4, 2, 1):
        pair = add(pair, rolled(pair, step, 0))
    return pair


def total_of(pairs):
    while len(pairs) > 1:
        pairs = [add(*pairs[k : k + 2]) if k + 1 < len(pairs) else pairs[k] for k in range(0, len(pairs), 2)]
    return pairs[0]


def middle_body(sums, out):
    pair = over_rows(total_of([(sums[k : k + 8], jnp.zeros((8, 128), F32)) for k in range(0, sums.shape[0], 8)]))
    high, low = add(pair, rolled(pair, 120, 1))
    line = jnp.where(iota(1, (8, 128)) % 16 < 8, high, pltpu.roll(low, 8, 1))
    for k in range(0, out.shape[0], 8):
        count = min(8, out.shape[0] - k)
        out[k : k + count] = line[0:count]


def final_body(sums, basis, own, table, displacement, viscous_next):
    pairs = []
    for k in range(sums.shape[0] // 8):
        tile = sums[8 * k : 8 * k + 8]
        pairs.append((tile, pltpu.roll(tile, 120, 1)))
    pair = over_rows(total_of(pairs))
    for step in (4, 2, 1):
        pair = add(pair, rolled(pair, 128 - step, 1))

    def moment(k):
        index = jnp.full((8, 128), 16 * k, jnp.int32)
        return tuple(jnp.take_along_axis(part, index, axis=1, mode="promise_in_bounds") for part in pair)

    moments = [moment(k) for k in range(MOMENTS)]
    matrix = [[moments[i + j + 1] for j in range(i + 1)] for i in range(ITERS)]
    value = moments[:ITERS]
    ratio = {}
    inverse = []
    for k in range(ITERS):
        pivot = matrix[k][k]
        kept = pivot[0] > TINY_PIVOT * moments[2 * k + 1][0]
        inverse.append(tuple(jnp.where(kept, part, 0.0) for part in invert(pivot)))
        for i in range(k + 1, ITERS):
            ratio[i, k] = multiply(matrix[i][k], inverse[k])
            for j in range(k + 1, i + 1):
                matrix[i][j] = subtract(matrix[i][j], multiply(ratio[i, k], matrix[j][k]))
            value[i] = subtract(value[i], multiply(ratio[i, k], value[k]))
    value = [multiply(value[k], inverse[k]) for k in range(ITERS)]
    for k in reversed(range(ITERS)):
        for i in range(k):
            value[i] = subtract(value[i], multiply(ratio[k, i], value[k]))
    weights = [SCALE * jnp.concatenate([v[0], v[0]], axis=0) for v in value]

    pairs = []
    for layer in range(3):
        fields = []
        for comp in range(3):
            total = weights[0] * basis[0, comp, layer]
            for step in range(1, ITERS):
                total = total + weights[step] * basis[step, comp, layer]
            if layer > 0:
                displacement[comp, layer - 1] = total[0:8]
            fields.append(node_pairs(total, last=False))
        pairs.append(fields)
    for layer in range(2):
        u, v, w = element_modes(pairs[layer], pairs[layer + 1])
        strain = (
            0.25 * u["dss"],
            0.25 * v["sds"],
            0.25 * w["ssd"],
            0.125 * (w["sds"] + v["ssd"]),
            0.125 * (w["dss"] + u["ssd"]),
            0.125 * (v["dss"] + u["sds"]),
        )
        index = own[18 + layer].astype(jnp.int32) + CLASSES
        entries = jnp.broadcast_to(table[3:4], (8, 128))
        retain = jnp.take_along_axis(entries, index, axis=1, mode="promise_in_bounds")
        for part in range(6):
            old = own[6 + 2 * part + layer]
            viscous_next[part, layer] = retain * old + (1.0 - retain) * strain[part][0:8]


def shifted(value, axes, count, steps):
    pairs = [(i, i + steps) for i in range(count) if 0 <= i + steps < count]
    return lax.ppermute(value, axes, pairs)


def swapped(value, axes, count, start):
    lower = [i for i in range(start, count - 1, 2)]
    return lax.ppermute(value, axes, [(i, i + 1) for i in lower] + [(i + 1, i) for i in lower])


def solution(mesh):
    count_x, count_z = mesh.shape["gx"], mesh.shape["gy"]
    along = min(8, count_x // 2)
    across = count_x // (2 * along)
    grid = Mesh(mesh.devices.reshape(across, along, 2, count_z), ("y", "x", "core", "z"))
    chips = along * across

    def shards(load, viscous, material, free_nodes, moduli_table, relax_time):
        def parity(axes):
            return (lax.axis_index(axes) % 2).astype(jnp.int32).reshape(1)

        odd_chip, core = parity("x"), parity("core")
        own, low, high, table = call(
            pack_body,
            (SDS((22, 8, 128), F32), SDS((11, 8, 128), F32), SDS((11, 8, 128), F32), SDS((8, 128), F32)),
            6,
            scratch=(
                pltpu.VMEM((2, 8, 128), jnp.int32),
                pltpu.VMEM((2, 8, 128), jnp.int32),
                pltpu.VMEM((3, CLASSES), F32),
                pltpu.VMEM((1, CLASSES), F32),
                pltpu.SemaphoreType.DMA((6,)),
            ),
            spec=HBM,
        )(
            *(
                pltpu.with_memory_space_constraint(value, pltpu.HBM)
                for value in (
                    load.reshape(6, 8, 128),
                    viscous.reshape(12, 8, 128),
                    material,
                    free_nodes,
                    moduli_table,
                    relax_time.reshape(1, CLASSES),
                )
            )
        )
        below = shifted(high, ("z",), count_z, 1)
        above = shifted(low, ("z",), count_z, -1)
        wide = call(widen_body, SDS((BLOCK, ROWS, 128), F32), 4)(own, above, below, table)
        first = swapped(wide, ("y", "x"), chips, 0)
        second = swapped(wide, ("y", "x"), chips, 1)
        given, sides = call(
            choose_body,
            (SDS((2, BLOCK, ROWS, 128), F32), SDS((2, BLOCK, ROWS, 128), F32)),
            5,
            scalars=2,
        )(core, odd_chip, wide, first, second)
        taken = lax.ppermute(given, ("core",), [(0, 1), (1, 0)])
        near, far = 2 * along, across * count_z
        basis, sums = call(
            krylov_body,
            (SDS((ITERS, 3, 3, ROWS, 128), F32), SDS((near, 128), F32)),
            4,
            scratch=(
                pltpu.VMEM((ITERS, 3, LAYERS, ROWS, 128), F32),
                pltpu.VMEM((LAYERS, ROWS, 128), F32),
                pltpu.VMEM((5, LAYERS, ROWS, 128), F32),
            ),
            flops=20000000,
        )(sides, taken, wide, table)
        group = lax.all_to_all(sums.reshape(near, 1, 128), ("x", "core"), 0, 0)
        partial = call(middle_body, SDS((far, 128), F32), 1)(group.reshape(near, 128))
        everything = lax.all_to_all(partial.reshape(far, 1, 128), ("y", "z"), 0, 0)
        return tuple(
            call(final_body, (SDS((3, 2, 8, 128), F32), SDS((6, 2, 8, 128), F32)), 4)(
                jnp.pad(everything.reshape(far, 128), ((0, -far % 8), (0, 0))), basis, own, table
            )
        )

    return jax.shard_map(
        shards,
        mesh=grid,
        in_specs=(
            P(None, ("y", "x", "core"), "z", None),
            P(None, ("y", "x", "core"), "z", None),
            P(("y", "x", "core"), "z", None),
            P(("y", "x", "core"), "z", None),
            P(),
            P(),
        ),
        out_specs=(P(None, ("y", "x", "core"), "z", None), P(None, ("y", "x", "core"), "z", None)),
        check_vma=False,
    )
```
